128 devices in a mesh: dp: 16 (over z, y), narrow: 8 (over x, core).
Axes of the slice: x: 4, y: 4, z: 4, core: 2. Of those that a mesh axis runs over, the one named last changes fastest.
Arguments:
- waveforms: float32 [256, 16000], P(('dp', 'narrow'))
- valid_counts: int32 [256], P(('dp', 'narrow')), may hold values from 0 to 16000, as said below
- balance_list: int32 [256], P(('dp', 'narrow')), may hold values from -1 to 7, as said below
- cotangent: bfloat16 [128, 49, 512], P(('dp', 'narrow')), may hold values from -0.52734375 to 0.52734375
- w_first: bfloat16 [10, 512], replicated, may hold values from -2 to 2
- w_three: bfloat16 [4, 3, 512, 512], replicated, may hold values from -0.15625 to 0.15625
- w_two: bfloat16 [2, 2, 512, 512], replicated, may hold values from -0.1875 to 0.1875
- conv_bias: float32 [7, 512], replicated, may hold values from -3 to 3
- norm_gain: float32 [7, 512], replicated, may hold values from 0.1 to 1.9
- norm_shift: float32 [7, 512], replicated, may hold values from -3 to 3
Outputs:
- grad_flat: float32 [4210176], P(('dp', 'narrow'))
The draws below stay inside these ranges and needn't reach their ends.
Inputs may be any that keep to these rules, and one draw needn't show every extreme that they name: `balance_list`: within each group of 8 devices sharing a dp index, exactly half of the group's slots are filled, and each of the group's 8 * 1 compute slots is named by exactly one filled slot; empty slots hold -1. `valid_counts`: 0 exactly on empty slots; filled slots hold at least 4000, and one filled slot of every group holds 16000.
All inputs are finite; a program needn't handle non-finite values.
Results may differ from the reference program's by a relative error of at most 0.02.
Values may be sent and summed in bfloat16 or wider, within the bound.
A program may use at most 192 MiB of HBM per device.

```python
import jax
import jax.numpy as jnp
from jax import lax

C = 512
S = 16000
B_DEV = 1
SLOTS = 256
BLOCKS = 128
F7 = 49
PARAMS = 4210176
PARAMS_PAD = 4210176
N_DP = 16
N_NARROW = 8


def balance_plan(key):
    group_size = N_NARROW * B_DEV
    per_group = 2 * group_size

    def one_group(group_key):
        order_key, length_key = jax.random.split(group_key)
        order = jax.random.permutation(order_key, per_group).astype(jnp.int32)
        ranks = jnp.arange(per_group, dtype=jnp.int32)
        dest_sorted = jnp.where(ranks < group_size, ranks, -1)
        drawn = jax.random.randint(length_key, (per_group,), S // 4, S + 1, dtype=jnp.int32)
        drawn = jnp.where(ranks == 0, S, drawn)
        drawn = jnp.where(ranks < group_size, drawn, 0)
        destination = jnp.zeros((per_group,), jnp.int32).at[order].set(dest_sorted)
        counted = jnp.zeros((per_group,), jnp.int32).at[order].set(drawn)
        return (destination, counted)
    destination, counted = jax.vmap(one_group)(jax.random.split(key, N_DP))
    return (destination.reshape(-1), counted.reshape(-1))


def draw_balance_list(key, part):
    destination, counted = balance_plan(key)
    return destination


def draw_valid_counts(key, part):
    destination, counted = balance_plan(key)
    return counted


def draw_waveforms(key, part):
    key = jax.random.fold_in(key, 7)
    noise_key, level_key = jax.random.split(key, 2)
    segments = S // 160
    levels = jnp.exp(jax.random.uniform(level_key, (SLOTS, segments, 1), jnp.float32, jnp.log(0.2), jnp.log(2.0)))
    noise = jax.random.normal(noise_key, (SLOTS, segments, 160), jnp.float32)
    return (jnp.clip(noise, -4.0, 4.0) * levels).reshape(SLOTS, S)


def block_levels(key, shape, cuts, smallest, largest):
    loudness, own = 1.0, jax.random.fold_in(key, 6)
    for position, blocks in cuts:
        heights = jnp.exp(jax.random.uniform(jax.random.fold_in(own, position), (blocks,), jnp.float32, smallest / len(cuts), largest / len(cuts)))
        loudness = loudness * jnp.repeat(heights, shape[position] // blocks).reshape([-1 if axis == position else 1 for axis in range(len(shape))])
    return loudness


def bell_draw(own_key, extent, scale, most, cuts=(), held_as=jnp.bfloat16):
    result = jax.random.normal(own_key, extent, jnp.float32) * scale
    if len(cuts) > 0:
        result = block_levels(own_key, extent, cuts, -0.22, 0.18) * result
    return jnp.clip(result, min=-most, max=most).astype(held_as)


def setup_inputs(seed: int = 0) -> dict:
    seeds = jax.random.split(jax.random.key(seed), 11)
    return {
        "waveforms": draw_waveforms(jax.random.fold_in(seeds[10], 71), 0),
        "valid_counts": draw_valid_counts(jax.random.fold_in(seeds[10], 71), 0),
        "balance_list": draw_balance_list(jax.random.fold_in(seeds[10], 71), 0),
        "cotangent": bell_draw(seeds[3], (BLOCKS, F7, C), ((N_DP * N_NARROW * B_DEV) ** -0.5), 0.52734375, ((0, 128),)),
        "w_first": bell_draw(seeds[4], (10, C), 10 ** -0.5, 2.0),
        "w_three": bell_draw(seeds[5], (4, 3, C, C), (3 * C) ** -0.5, 0.15625),
        "w_two": bell_draw(seeds[6], (2, 2, C, C), (2 * C) ** -0.5, 0.1875),
        "conv_bias": bell_draw(seeds[7], (7, C), 0.5, 3.0, (), jnp.float32),
        "norm_gain": jnp.clip(1.0 + 0.18 * jax.random.normal(seeds[8], (7, C), jnp.float32), 0.1, 1.9),
        "norm_shift": bell_draw(seeds[9], (7, C), 0.5, 3.0, (), jnp.float32),
    }


layer_plan = ((10, 5), (3, 2), (3, 2), (3, 2), (3, 2), (2, 2), (2, 2))

def contract(form, left, right):
    return jnp.einsum(form, left.astype(jnp.float32), right.astype(jnp.float32))

def layer_weight(w_first, w_three, w_two, layer):
    if layer == 0:
        return w_first[:, None, :]
    if layer < 5:
        return w_three[layer - 1]
    return w_two[layer - 5]

def post_conv(conv_out, bias_row, gain_row, shift_row):
    shifted = conv_out + bias_row
    average = lax.optimization_barrier(jnp.mean(shifted, axis=-1, keepdims=True))
    centred = shifted - average
    spread = lax.optimization_barrier(jnp.mean(centred * centred, axis=-1, keepdims=True))
    normed = centred * lax.rsqrt(spread + 1e-05) * gain_row + shift_row
    return jax.nn.gelu(normed, approximate=False)

def split_weight(weight, stride):
    kernel, in_width, width = weight.shape
    w_head = weight[:stride].reshape(stride * in_width, width)
    w_tail = None
    if kernel > stride:
        w_tail = jnp.pad(weight[stride:], ((0, 2 * stride - kernel), (0, 0), (0, 0))).reshape(stride * in_width, width)
    return (w_head, w_tail)

def forward_layer(inputs, weight, stride):
    batch_size, length, in_width = inputs.shape
    kernel = weight.shape[0]
    frames = (length - kernel) // stride + 1
    row_count = (frames + 1) * stride
    trimmed = inputs[:, :min(length, row_count)]
    trimmed = jnp.pad(trimmed, ((0, 0), (0, row_count - trimmed.shape[1]), (0, 0)))
    packed = trimmed.reshape(batch_size, frames + 1, stride * in_width)
    w_head, w_tail = split_weight(weight, stride)
    conv_out = contract('btk,kc->btc', packed[:, :frames], w_head)
    if w_tail is not None:
        conv_out = conv_out + contract('btk,kc->btc', packed[:, 1:], w_tail)
    return (conv_out, packed)

def backward_layer(grad_out, conv_out, packed, weight, stride, bias_row, gain_row, shift_row, length, need_input):
    kernel, in_width, width = weight.shape
    frames = conv_out.shape[1]
    batch_size = conv_out.shape[0]
    unused, pullback = jax.vjp(post_conv, conv_out, bias_row, gain_row, shift_row)
    grad_conv, grad_bias, grad_gain, grad_shift = pullback(grad_out.astype(jnp.float32))
    grad_low = grad_conv.astype(jnp.bfloat16)
    pieces = [contract('btk,btc->kc', packed[:, :frames], grad_low).reshape(stride, in_width, width)]
    if kernel > stride:
        pieces.append(contract('btk,btc->kc', packed[:, 1:], grad_low).reshape(stride, in_width, width)[:kernel - stride])
    grad_weight = jnp.concatenate(pieces, axis=0)
    grad_input = None
    if need_input:
        w_head, w_tail = split_weight(weight, stride)
        scattered = jnp.pad(contract('btc,kc->btk', grad_low, w_head), ((0, 0), (0, 1), (0, 0)))
        if w_tail is not None:
            scattered = scattered + jnp.pad(contract('btc,kc->btk', grad_low, w_tail), ((0, 0), (1, 0), (0, 0)))
        grad_input = scattered.reshape(batch_size, (frames + 1) * stride, in_width)[:, :length].astype(jnp.bfloat16)
    return (grad_weight, grad_bias, grad_gain, grad_shift, grad_input)

def normalize_wave(waveforms, lengths):
    positions = jnp.arange(waveforms.shape[1], dtype=jnp.int32)
    valid = (positions[None, :] < lengths[:, None]).astype(jnp.float32)
    divisor = jnp.maximum(lengths, 1).astype(jnp.float32)
    average = lax.optimization_barrier(jnp.sum(waveforms * valid, axis=1)) / divisor
    centred = (waveforms - average[:, None]) * valid
    spread = lax.optimization_barrier(jnp.sum(centred * centred, axis=1)) / divisor
    return (centred * lax.rsqrt(spread + 1e-07)[:, None]).astype(jnp.bfloat16)[:, :, None]

def encoder_grads(waveforms, lengths, grad_feat, w_first, w_three, w_two, conv_bias, norm_gain, norm_shift, padding):
    inputs = normalize_wave(waveforms, lengths)
    saved = []
    frame_len = lengths
    for layer in range(7):
        kernel, stride = layer_plan[layer]
        weight = layer_weight(w_first, w_three, w_two, layer)
        conv_out, packed = forward_layer(inputs, weight, stride)
        saved.append((conv_out, packed, inputs.shape[1]))
        inputs = post_conv(conv_out, conv_bias[layer], norm_gain[layer], norm_shift[layer]).astype(jnp.bfloat16)
        frame_len = (frame_len - kernel) // stride + 1
    positions = jnp.arange(grad_feat.shape[1], dtype=jnp.int32)
    frame_mask = (positions[None, :] < frame_len[:, None]).astype(jnp.bfloat16)
    grad_out = grad_feat * frame_mask[:, :, None]
    weight_grads = [None] * 7
    bias_grads = [None] * 7
    gain_grads = [None] * 7
    shift_grads = [None] * 7
    for layer in range(6, -1, -1):
        kernel, stride = layer_plan[layer]
        weight = layer_weight(w_first, w_three, w_two, layer)
        conv_out, packed, length = saved[layer]
        outcome = backward_layer(grad_out, conv_out, packed, weight, stride, conv_bias[layer], norm_gain[layer], norm_shift[layer], length, layer > 0)
        weight_grads[layer], bias_grads[layer], gain_grads[layer], shift_grads[layer], grad_out = outcome
    pieces = [weight_grads[0].reshape(-1)]
    pieces += [weight_grads[layer].reshape(-1) for layer in range(1, 7)]
    pieces += [jnp.stack(bias_grads).reshape(-1), jnp.stack(gain_grads).reshape(-1), jnp.stack(shift_grads).reshape(-1)]
    pieces.append(jnp.zeros((padding,), jnp.float32))
    return jnp.concatenate(pieces)

def reference(waveforms, valid_counts, balance_list, cotangent, w_first, w_three, w_two, conv_bias, norm_gain, norm_shift):
    group_size = N_NARROW * B_DEV
    slot_ids = jnp.arange(SLOTS, dtype=jnp.int32)
    group_of = slot_ids // (2 * group_size)
    target = jnp.where(balance_list >= 0, group_of * group_size + balance_list, BLOCKS).astype(jnp.int32)
    source = jnp.zeros((BLOCKS + 1,), jnp.int32).at[target].set(slot_ids)[:BLOCKS]
    padding = PARAMS_PAD - PARAMS

    def advance(summed, device):
        block_ids = (device * B_DEV + jnp.arange(B_DEV, dtype=jnp.int32)).astype(jnp.int32)
        chosen = source[block_ids]
        waves_here = jnp.take(waveforms, chosen, axis=0)
        counts_here = jnp.take(valid_counts, chosen, axis=0)
        grad_feat = lax.dynamic_slice_in_dim(cotangent, (device * B_DEV).astype(jnp.int32), B_DEV, 0)
        flat_grads = encoder_grads(waves_here, counts_here, grad_feat, w_first, w_three, w_two, conv_bias, norm_gain, norm_shift, padding)
        return (summed + flat_grads, None)
    summed, unused = lax.scan(advance, jnp.zeros((PARAMS_PAD,), jnp.float32), jnp.arange(N_DP * N_NARROW, dtype=jnp.int32))
    return summed
```

```python
import jax
import jax.numpy as jnp
from jax import lax
from jax.experimental import pallas as pl
from jax.experimental.pallas import tpu as pltpu
from jax.sharding import PartitionSpec as P

C = 512
F7 = 49
BF = jnp.bfloat16
F32 = jnp.float32

taps = (None, 3, 3, 3, 3, 2, 2)
phases = (8, 4, 2, 1, 1, 1, 1)
rows_of = (400, 400, 400, 400, 208, 112, 64)
in_blocks = (None, 9, 5, 3, 3, 2, 2)
ROW_TILE = {400: 400, 208: 208, 112: 112, 64: 64}


def dot(a, b):
    return jnp.dot(a, b, preferred_element_type=F32)


def dot_bt(a, b):
    return lax.dot_general(a, b, (((1,), (1,)), ((), ())), preferred_element_type=F32)


def dot_at(a, b):
    return lax.dot_general(a, b, (((0,), (0,)), ((), ())), preferred_element_type=F32)


def gelu_pair(n):
    e = jnp.exp(n * n * -0.5)
    t = 1.0 / (1.0 + jnp.abs(n) * (0.3275911 * 0.7071067811865476))
    poly = 0.5 * 1.061405429
    for a in (-1.453152027, 1.421413741, -0.284496736, 0.254829592):
        poly = poly * t + 0.5 * a
    half = poly * t * e
    phi = jnp.where(n >= 0, 1.0 - half, half)
    x = n * phi
    return x, phi + (n * 0.3989422804014327) * e


def loop_rows(rows, body, init):
    tile = ROW_TILE[rows]

    def step(i, carry):
        return body(pl.ds(pl.multiple_of(i * tile, tile), tile), carry)

    return lax.fori_loop(0, rows // tile, step, init)


def fold8(v):
    total = v[0:8]
    for i in range(8, v.shape[0], 8):
        total = total + v[i : i + 8]
    return total


def encoder_body(
    route, cot, w1, w3_hbm, w2_hbm, bias, gain, shift,
    emit, between, small,
    a0, w3, w2, wb, gw, x_refs, dg_refs, xh_refs, rs_refs, zs, zt, fs, f4, dz, gn, acc, bb, mm, bandf, wsem,
):
    w_copies = []
    for i in range(4):
        w_copies.append(pltpu.make_async_copy(w3_hbm.at[i], w3.at[i], wsem.at[i]))
    for i in range(2):
        w_copies.append(pltpu.make_async_copy(w2_hbm.at[i], w2.at[i], wsem.at[4 + i]))
    for c in w_copies:
        c.start()

    def weight(l, k):
        if l < 5:
            return w3[l - 1, k * C : (k + 1) * C, :]
        return w2[l - 5, k * C : (k + 1) * C, :]

    wf = w1[...].astype(F32)
    wc = wf - jnp.mean(wf, axis=-1, keepdims=True)
    b0 = bias[0:1, :]
    bc = b0 - jnp.mean(b0, axis=-1, keepdims=True)
    g0 = gain[0:1, :]

    def split(v):
        hi = v.astype(BF).astype(F32)
        return hi, v - hi

    wc_hi, wc_lo = split(wc)
    bc_hi, bc_r = split(bc)
    bc_mid, bc_lo = split(bc_r)
    gw_hi, gw_lo = split(wc * g0)
    gb_hi, gb_lo = split(bc * g0)
    g_hi, g_lo = split(g0)
    for p in range(8):
        bandf[...] = jnp.zeros_like(bandf)
        bandf[5 * p : 5 * p + 10, :] = wc_hi
        bandf[45 + 5 * p : 55 + 5 * p, :] = wc_lo
        bandf[90:91, :] = bc_hi
        bandf[91:92, :] = bc_mid
        bandf[92:93, :] = bc_lo
        wb[:, p * C : (p + 1) * C] = bandf[...].astype(BF)
        bandf[5 * p : 5 * p + 10, :] = gw_hi
        bandf[45 + 5 * p : 55 + 5 * p, :] = gw_lo
        bandf[90:91, :] = gb_hi
        bandf[91:92, :] = gb_lo
        bandf[92:93, :] = jnp.zeros_like(bc_lo)
        bandf[126:127, :] = g_hi
        bandf[127:128, :] = g_lo
        gw[:, p * C : (p + 1) * C] = bandf[...].astype(BF)

    fs[400:424, :] = jnp.zeros((24, C), F32)
    f4[:, 400:424, :] = jnp.zeros((4, 24, 128), F32)

    last_frames = route()

    def activate(l, p, centred):
        rows = rows_of[l]
        lanes = pl.ds(pl.multiple_of(p * C, C), C)
        b = bias[l : l + 1, :]
        g = gain[l : l + 1, :]
        s = shift[l : l + 1, :]

        def body(r, carry):
            z = zs[r, :]
            if not centred:
                z = z + b
                z = z - jnp.sum(z, axis=-1, keepdims=True) * (1.0 / C)
            var = jnp.sum(z * z, axis=-1, keepdims=True) * (1.0 / C)
            rstd = lax.rsqrt(var + 1e-05)
            xh = z * rstd
            x, d = gelu_pair(xh * g + s)
            dg_refs[l][r, lanes] = d.astype(BF)
            if l > 0:
                xh_refs[l][r, lanes] = xh.astype(BF)
            rs_refs[l][p, r, :] = jnp.broadcast_to(rstd, (rstd.shape[0], 128))
            if l < 3:
                x_refs[l + 1][r, lanes] = x.astype(BF)
            if l < 3:
                fs[r, :] = x
            elif l < 6:
                for c in range(4):
                    f4[c, r, :] = x[:, c * 128 : (c + 1) * 128]
            return carry

        loop_rows(rows, body, 0)
        if l < 3:
            @pl.when(p == 0)
            def _():
                n = phases[l]
                x_refs[l + 1][:, n * C : (n + 1) * C] = fs[pl.ds(1, 400), :].astype(BF)

    def first(p, carry):
        lanes = pl.ds(pl.multiple_of(p * C, C), C)
        zs[...] = dot(a0[...], wb[:, lanes])
        activate(0, p, True)
        return carry

    lax.fori_loop(0, 8, first, 0)

    for l in range(1, 7):
        w_copies[l - 1].wait()
        k, rows = taps[l], rows_of[l]

        def conv(p, carry, l=l, k=k, rows=rows):
            x = x_refs[l][:, pl.ds(pl.multiple_of(p * 2 * C, 2 * C), k * C)]
            w = w3[l - 1] if l < 5 else w2[l - 5]
            zs[0:rows, :] = dot(x, w)
            activate(l, p, False)
            return carry

        if phases[l] > 1:
            lax.fori_loop(0, phases[l], conv, 0)
        else:
            conv(0, 0)
        if 3 <= l < 6:
            n = rows_of[l + 1]
            for j in range(taps[l + 1]):
                for c in range(4):
                    x_refs[l + 1][:, j * C + c * 128 : j * C + (c + 1) * 128] = f4[
                        c, pl.ds(j, n, stride=2), :
                    ].astype(BF)

    row_id = lax.broadcasted_iota(jnp.int32, (F7, C), 0).astype(F32)
    zs[0:64, :] = jnp.zeros((64, C), F32)
    zs[0:F7, :] = jnp.where(row_id < last_frames, cot[0].astype(F32), 0.0)

    def got(src, r):
        if src is None:
            return jnp.concatenate([f4[c, r, :] for c in range(4)], axis=-1)
        return src[r, :]

    def norm_back(l, p, src, sums):
        lanes = pl.ds(pl.multiple_of(p * C, C), C)
        out = pl.ds(pl.multiple_of((p + 1) * C, C), C)
        g = gain[l : l + 1, :]

        def body(r, carry):
            db, dga, dsh = carry
            gv = got(src, r) * dg_refs[l][r, lanes].astype(F32)
            xh = xh_refs[l][r, lanes].astype(F32)
            rstd = rs_refs[l][p, r, :][:, 0:1]
            dsh = dsh + fold8(gv)
            dga = dga + fold8(gv * xh)
            gx = gv * g
            m1 = jnp.sum(gx, axis=-1, keepdims=True) * (1.0 / C)
            m2 = jnp.sum(gx * xh, axis=-1, keepdims=True) * (1.0 / C)
            d = (gx - m1 - xh * m2) * rstd
            db = db + fold8(d)
            dz[r, out] = d.astype(BF)
            return db, dga, dsh

        return loop_rows(rows_of[l], body, sums)

    zero8 = jnp.zeros((8, C), F32)
    sums = norm_back(6, 0, zs, (zero8, zero8, zero8))

    def store_sums(l, sums):
        for j in range(3):
            small[10 + 7 * j + l : 11 + 7 * j + l, :] = jnp.sum(sums[j], axis=0, keepdims=True)

    for l in range(6, 0, -1):
        k, rows, n = taps[l], rows_of[l], phases[l]
        store_sums(l, sums)
        if k == 3:
            fs[8 : 8 + rows, :] = dz[0:rows, n * C : (n + 1) * C].astype(F32)
            fs[0:8, :] = jnp.zeros((8, C), F32)
            dz[0:rows, 0:C] = fs[pl.ds(7, rows), :].astype(BF)

        def wgrad(p, carry, l=l, k=k, rows=rows):
            x = x_refs[l][:, pl.ds(pl.multiple_of(p * 2 * C, 2 * C), k * C)]
            d = dz[0:rows, pl.ds(pl.multiple_of((p + 1) * C, C), C)]
            for j in range(k):
                part = dot_at(x[:, j * C : (j + 1) * C], d)
                if isinstance(p, int):
                    acc[j * C : (j + 1) * C, :] = part
                else:
                    acc[j * C : (j + 1) * C, :] += part
            return carry

        wgrad(0, 0)
        if n > 1:
            lax.fori_loop(1, n, wgrad, 0)
        emit(l, acc)

        if l > 3:
            here = dz[0:rows, C : 2 * C]
            even = dot_bt(here, weight(l, 0))
            if k == 3:
                even = even + dot_bt(dz[0:rows, 0:C], weight(l, 2))
            odd = dot_bt(here, weight(l, 1))
            half = rows_of[l - 1] // 2
            for c in range(4):
                f4[c, pl.ds(0, half, stride=2), :] = even[:half, c * 128 : (c + 1) * 128]
                f4[c, pl.ds(1, half, stride=2), :] = odd[:half, c * 128 : (c + 1) * 128]
            sums = norm_back(l - 1, 0, None, (zero8, zero8, zero8))
            between(l)
        elif l > 1:
            def dgrad(p, carry, l=l):
                here = dz[:, pl.ds(pl.multiple_of((p + 1) * C, C), C)]
                before = dz[:, pl.ds(pl.multiple_of(p * C, C), C)]
                zt[2 * p] = dot_bt(here, weight(l, 0)) + dot_bt(before, weight(l, 2))
                zt[2 * p + 1] = dot_bt(here, weight(l, 1))
                return carry

            for p in range(n):
                dgrad(p, 0)

            def back(p, carry, l=l):
                return norm_back(l - 1, p, zt.at[p], carry)

            sums = lax.fori_loop(0, 2 * n, back, (zero8, zero8, zero8))
            between(l)
        else:
            def first_back(p, dsh):
                def one(q, src, dsh):
                    lanes = pl.ds(pl.multiple_of(q * C, C), C)
                    zs[...] = src

                    def body(r, dsh):
                        gv = zs[r, :] * dg_refs[0][r, lanes].astype(F32)
                        dsh = dsh + fold8(gv)
                        gn[r, 0:C] = (gv * rs_refs[0][q, r, :][:, 0:1]).astype(BF)
                        return dsh

                    dsh = loop_rows(400, body, dsh)
                    u = dot_bt(gn[:, 0:C], gw[:, lanes])
                    a = a0[...].astype(F32)
                    lane = lax.broadcasted_iota(jnp.int32, (400, 128), 1)
                    m2 = jnp.sum(a * u, axis=-1, keepdims=True) * (1.0 / C)
                    m1 = jnp.sum(jnp.where(lane >= 126, u, 0.0), axis=-1, keepdims=True) * (1.0 / C)
                    rstd = rs_refs[0][q]
                    rhs = jnp.where(lane == 127, m1, a * (rstd * rstd * m2))
                    hi = rhs.astype(BF)
                    gn[:, C : C + 128] = hi
                    gn[:, C + 128 : C + 256] = (rhs - hi.astype(F32)).astype(BF)
                    both = dot_at(a0[...], gn[...])
                    bb[lax.rem(q, 4), pl.ds(pl.multiple_of(lax.div(q, 4) * 128, 128), 128), :] = both[:, 0:C]
                    mm[q] = both[:, C : C + 128] + both[:, C + 128 : C + 256]
                    return dsh

                here = dz[:, pl.ds(pl.multiple_of((p + 1) * C, C), C)]
                before = dz[:, pl.ds(pl.multiple_of(p * C, C), C)]
                dsh = one(2 * p, dot_bt(here, weight(1, 0)) + dot_bt(before, weight(1, 2)), dsh)
                dsh = one(2 * p + 1, dot_bt(here, weight(1, 1)), dsh)
                for i in range(4):
                    @pl.when(p == i)
                    def _(i=i):
                        between(("first", i))
                return dsh

            dsh = lax.fori_loop(0, 4, first_back, zero8)
            dw = jnp.zeros((10, C), F32)
            db = jnp.zeros((1, C), F32)
            dga = jnp.zeros((1, C), F32)
            for q in range(8):
                bq = bb[q % 4, q // 4 * 128 : q // 4 * 128 + 128, :]
                band = wb[:, q * C : (q + 1) * C].astype(F32)
                dga = dga + jnp.sum(bq * band, axis=0, keepdims=True)
                m = mm[q]
                bandf[...] = bq * g0 - m[:, 127:128] - jnp.dot(
                    m, band, preferred_element_type=F32, precision=lax.Precision.HIGHEST
                )
                dw = dw + bandf[5 * q : 5 * q + 10, :]
                db = db + bandf[90:91, :]
            small[0:10, :] = dw
            small[10:11, :] = db
            small[17:18, :] = dga
            small[24:25, :] = jnp.sum(dsh, axis=0, keepdims=True)
            small[31:32, :] = jnp.zeros((1, C), F32)


def body_scratch():
    s = [
        pltpu.VMEM((400, 128), BF),
        pltpu.VMEM((4, 3 * C, C), BF),
        pltpu.VMEM((2, 2 * C, C), BF),
        pltpu.VMEM((128, 8 * C), BF),
        pltpu.VMEM((128, 8 * C), BF),
    ]
    s.append([pltpu.VMEM((rows_of[l], in_blocks[l] * C), BF) for l in range(1, 7)])
    s.append([pltpu.VMEM((rows_of[l], phases[l] * C), BF) for l in range(7)])
    s.append([pltpu.VMEM((rows_of[l], phases[l] * C), BF) for l in range(1, 7)])
    s.append([pltpu.VMEM((phases[l], rows_of[l], 128), F32) for l in range(7)])
    s += [
        pltpu.VMEM((400, C), F32),
        pltpu.VMEM((4, 400, C), F32),
        pltpu.VMEM((424, C), F32),
        pltpu.VMEM((4, 424, 128), F32),
        pltpu.VMEM((400, 5 * C), BF),
        pltpu.VMEM((400, C + 256), BF),
        pltpu.VMEM((3 * C, C), F32),
        pltpu.VMEM((8, 128, 128), F32),
        pltpu.VMEM((128, C), F32),
        pltpu.SemaphoreType.DMA((6,)),
    ]
    return s


MESH = pl.DeviceIdType.MESH
SHARD = 32892
ORDERS = (("x", "y", "z"), ("y", "z", "x"), ("z", "x", "y"))


def unit_of(l, k):
    return (l - 1) * 3 + k if l < 5 else 12 + (l - 5) * 2 + k


def order_of(l, k):
    return ORDERS[(k + (2 if l == 6 else 0)) % 3]


def first_tile(d):
    return lax.div(SHARD * d + 3072, 8192) - 1


def encoder_kernel(
    packed, bal, cot, w1, w3_hbm, w2_hbm, bias, gain, shift, out, *scratch
):
    (a0, w3, w2, wb, gw, xs, dgs, xhs, rss, zs, zt, fs, f4, dz, gn, acc, mm, bandf, wsem,
     small, sb, rb, xr, s0, keep, r0, r1, h2, r2, h3, r3, tl, own, fl, rs0, hs, rs1, ts, root, root0, sm4,
     sb_sem, rb_sem, s0_sem, r0_sem, s1_sem, r1_sem, s2_sem, r2_sem, s3_sem, r3_sem, t_sem, own_sem,
     q_send, q_recv, root_sem, qr_send) = scratch

    dp = lax.axis_index("dp")
    nw = lax.axis_index("narrow")
    z, y = lax.div(dp, 4), lax.rem(dp, 4)
    x, core = lax.div(nw, 2), lax.rem(nw, 2)
    me = dp * 8 + nw
    at = {"x": x, "y": y, "z": z}

    def peer(axis, delta):
        if axis == "core":
            return (dp, x * 2 + (1 - core))
        if axis == "x":
            return (dp, lax.rem(x + delta, 4) * 2 + core)
        if axis == "y":
            return (z * 4 + lax.rem(y + delta, 4), nw)
        return (lax.rem(z + delta, 4) * 4 + y, nw)

    def remote(src, dst, send, recv, device):
        return pltpu.make_async_remote_copy(
            src_ref=src, dst_ref=dst, send_sem=send, recv_sem=recv, device_id=device, device_id_type=MESH
        )

    barrier = pltpu.get_barrier_semaphore()
    for d in range(1, 8):
        pl.semaphore_signal(barrier, inc=1, device_id=(dp, lax.rem(nw + d, 8)), device_id_type=MESH)
    for axis in ("y", "z"):
        for d in range(1, 4):
            pl.semaphore_signal(barrier, inc=1, device_id=peer(axis, d), device_id_type=MESH)

    def route():
        for d in range(8):
            there = lax.rem(nw + d, 8)
            m0 = jnp.where(bal[0] == there, 1.0, 0.0)
            m1 = jnp.where(bal[1] == there, 1.0, 0.0)
            sb[d] = (packed[0].astype(F32) * m0 + packed[1].astype(F32) * m1).astype(BF)
        pl.semaphore_wait(barrier, 13)
        copies = []
        for d in range(1, 8):
            c = remote(sb.at[d], rb.at[d - 1], sb_sem.at[d - 1], rb_sem.at[d - 1], (dp, lax.rem(nw + d, 8)))
            c.start()
            copies.append(c)
        g = sb[0].astype(F32)
        for d in range(1, 8):
            copies[d - 1].wait()
            g = g + rb[d - 1].astype(F32)
        for b in range(3):
            xr[144 * b : 144 * b + 144, :] = g if b == 0 else pltpu.roll(g, 128 - 40 * b, 1)
        xr[432:440, :] = jnp.zeros((8, 128), F32)
        v0 = xr[0:400, :]
        v1 = pltpu.roll(xr[pl.ds(1, 400), :], 40, 1)
        lane = lax.broadcasted_iota(jnp.int32, (400, 128), 1)
        one = jnp.where(lane < 40, v0, jnp.where(lane < 45, v1, 0.0))
        ones = jnp.where((lane >= 90) & (lane < 93), 1.0, 0.0)
        a0[...] = (one + pltpu.roll(one, 45, 1) + ones).astype(BF)
        return g[0:1, 127:128]

    def units(l):
        return [(k, unit_of(l, k), order_of(l, k)) for k in range(taps[l])]

    def slot(l, k):
        return (l % 2) * 3 + k

    def copy0(l, k, u):
        return remote(s0.at[slot(l, k)], r0.at[u], s0_sem.at[u], r0_sem.at[u], peer("core", 1))

    def move0(l, acc):
        for k, u, o in units(l):
            if l + 2 <= 6 and k < taps[l + 2]:
                copy0(l + 2, k, unit_of(l + 2, k)).wait_send()
            keep[u] = acc[pl.ds(pl.multiple_of(k * C + core * 256, 256), 256), :].astype(BF)
            s0[slot(l, k)] = acc[pl.ds(pl.multiple_of(k * C + (1 - core) * 256, 256), 256), :].astype(BF)
            copy0(l, k, u).start()

    def rows64(j):
        return pl.ds(pl.multiple_of(j * 64, 64), 64)

    def rows16(j):
        return pl.ds(pl.multiple_of(j * 16, 16), 16)

    def move1(l):
        for k, u, o in units(l):
            copy0(l, k, u).wait_recv()
            keep[u] = (keep[u].astype(F32) + r0[u].astype(F32)).astype(BF)
            for d in range(1, 4):
                j = lax.rem(at[o[0]] + d, 4)
                remote(keep.at[u, rows64(j)], r1.at[u, d - 1], s1_sem.at[u], r1_sem.at[u], peer(o[0], d)).start()

    def whole(ref, send, recv, o):
        return remote(ref, ref, send, recv, peer(o, 1))

    def move2(l):
        for k, u, o in units(l):
            whole(r1.at[u], s1_sem.at[u], r1_sem.at[u], o[0]).wait_recv()
            v = keep[u, rows64(at[o[0]]), :].astype(F32)
            for d in range(3):
                v = v + r1[u, d].astype(F32)
            h2[u] = v.astype(BF)
            for d in range(1, 4):
                j = lax.rem(at[o[1]] + d, 4)
                remote(h2.at[u, rows16(j)], r2.at[u, d - 1], s2_sem.at[u], r2_sem.at[u], peer(o[1], d)).start()

    def move3(l):
        for k, u, o in units(l):
            whole(r2.at[u], s2_sem.at[u], r2_sem.at[u], o[1]).wait_recv()
            v = h2[u, rows16(at[o[1]]), :].astype(F32)
            for d in range(3):
                v = v + r2[u, d].astype(F32)
            for c in range(4):
                h3[u, c] = v[:, c * 128 : (c + 1) * 128].astype(BF)
            for d in range(1, 4):
                j = lax.rem(at[o[2]] + d, 4)
                remote(h3.at[u, j], r3.at[u, d - 1], s3_sem.at[u], r3_sem.at[u], peer(o[2], d)).start()

    def owners(u, o):
        tile = u * 32 + core * 16 + at[o[0]] * 4 + at[o[1]]
        start = (10 + 16 * tile) * C
        first = lax.div(start, SHARD)
        last = lax.div(start + 8191, SHARD)
        return tile, ((first, True), (last, last != first))

    def final(u, o, i, tile, d):
        s = tile - first_tile(d)
        device = (lax.div(d, 8), lax.rem(d, 8))
        return remote(tl.at[u], own.at[s * 4 + at[o[2]]], t_sem.at[u, i], own_sem.at[s], device)

    def final_here(u, o, tile, d):
        s = tile - first_tile(d)
        return pltpu.make_async_copy(tl.at[u], own.at[s * 4 + at[o[2]]], own_sem.at[s])

    def move4(l):
        for k, u, o in units(l):
            whole(r3.at[u], s3_sem.at[u], r3_sem.at[u], o[2]).wait_recv()
            v = h3[u, at[o[2]]].astype(F32)
            for d in range(3):
                v = v + r3[u, d].astype(F32)
            tl[u] = v
            tile, targets = owners(u, o)
            for i, (d, wanted) in enumerate(targets):
                @pl.when(jnp.logical_and(wanted, d != me))
                def _(u=u, o=o, i=i, tile=tile, d=d):
                    final(u, o, i, tile, d).start()

                @pl.when(jnp.logical_and(wanted, d == me))
                def _(u=u, o=o, tile=tile, d=d):
                    final_here(u, o, tile, d).start()

    moves = (None, move1, move2, move3, move4)

    def emit(l, acc):
        move0(l, acc)
        for stage in range(1, 5):
            if l > 2 and l + stage <= 6:
                moves[stage](l + stage)
        if l == 2:
            for stage in range(1, 5):
                moves[stage](2 + stage)
        if l == 1:
            move2(2)
            move3(3)
            move4(4)

    def between(point):
        if point == 2:
            move1(2)
            move2(3)
            move3(4)
            move4(5)
        elif isinstance(point, tuple):
            i = point[1]
            if i == 0:
                move1(1)
                move3(2)
                move4(3)
            elif i == 1:
                move2(1)
                move4(2)
            elif i == 2:
                move3(1)
            else:
                move4(1)

    fl[...] = jnp.zeros_like(fl)
    encoder_body(
        route, cot, w1, w3_hbm, w2_hbm, bias, gain, shift, emit, between, small,
        a0, w3, w2, wb, gw, [None] + list(xs), list(dgs), [None] + list(xhs), list(rss),
        zs, zt, fs, f4, dz, gn, acc, zt, mm, bandf, wsem,
    )

    def rows_of_core(c):
        return pl.ds(pl.multiple_of(c * 16, 16), 16)

    c0 = remote(small.at[rows_of_core(1 - core)], rs0, q_send.at[0], q_recv.at[0], peer("core", 1))
    c0.start()
    c0.wait()
    v = small[rows_of_core(core), :] + rs0[...]
    for c in range(4):
        hs[c] = v[:, c * 128 : (c + 1) * 128]
    cx = []
    for d in range(1, 4):
        c1 = remote(hs.at[lax.rem(x + d, 4)], rs1.at[d - 1], q_send.at[d], q_recv.at[d], peer("x", d))
        c1.start()
        cx.append(c1)
    v = hs[x]
    for d in range(3):
        cx[d].wait()
        v = v + rs1[d]
    ts[...] = v
    to_last = remote(ts, root.at[me], qr_send.at[0], root_sem.at[0], (15, 7))
    my_last = pltpu.make_async_copy(ts, root.at[me], root_sem.at[0])
    to_zero = remote(ts, root0.at[dp * 4 + x], qr_send.at[1], root_sem.at[1], (0, 0))
    my_zero = pltpu.make_async_copy(ts, root0.at[dp * 4 + x], root_sem.at[1])
    is_last = me == 127
    is_zero = me == 0

    @pl.when(jnp.logical_not(is_last))
    def _():
        to_last.start()

    @pl.when(is_last)
    def _():
        my_last.start()

    @pl.when(jnp.logical_and(core == 0, jnp.logical_not(is_zero)))
    def _():
        to_zero.start()

    @pl.when(is_zero)
    def _():
        my_zero.start()

    low = first_tile(me)
    high = jnp.minimum(lax.div(SHARD * me + SHARD - 1 + 3072, 8192) - 1, 511)

    for s in range(6):
        @pl.when(jnp.logical_and(low + s >= 0, low + s <= high))
        def _(s=s):
            block = own.at[4 * s : 4 * s + 4]
            pltpu.make_async_copy(block, block, own_sem.at[s]).wait()
            for c in range(4):
                fl[pl.ds(64 * s + c, 16, stride=4), :] = own[4 * s + c]

    @pl.when(is_last)
    def _():
        pltpu.make_async_copy(root, root, root_sem.at[0]).wait()
        for c in range(4):
            for h in range(2):
                v = root[2 * c + h]
                for i in range(1, 16):
                    v = v + root[8 * i + 2 * c + h]
                sm4[c, 16 * h : 16 * h + 16, :] = v
            fl[pl.ds(192 + c, 21, stride=4), :] = sm4[c, 10:31, :]

    @pl.when(is_zero)
    def _():
        pltpu.make_async_copy(root0, root0, root_sem.at[1]).wait()
        for c in range(4):
            v = root0[c]
            for i in range(1, 16):
                v = v + root0[4 * i + c]
            sm4[c, 0:16, :] = v
            fl[pl.ds(24 + c, 10, stride=4), :] = sm4[c, 0:10, :]

    offset = SHARD * me - C * (10 + 16 * low)
    row = lax.div(offset, 128)
    turn = lax.rem(offset, 128)
    back = lax.rem(128 - turn, 128)
    upper = pltpu.roll(fl[pl.ds(row, 264), :], back, 1)
    lower = pltpu.roll(fl[pl.ds(row + 1, 264), :], back, 1)
    lane = lax.broadcasted_iota(jnp.int32, (264, 128), 1)
    out[...] = jnp.where(lane < 128 - turn, upper, lower)

    for l in range(1, 7):
        for k, u, o in units(l):
            if l <= 2:
                copy0(l, k, u).wait_send()
            elif k >= taps[l - 2]:
                copy0(l, k, u).wait_send()
            whole(r1.at[u], s1_sem.at[u], r1_sem.at[u], o[0]).wait_send()
            whole(r2.at[u], s2_sem.at[u], r2_sem.at[u], o[1]).wait_send()
            whole(r3.at[u], s3_sem.at[u], r3_sem.at[u], o[2]).wait_send()
            tile, targets = owners(u, o)
            for i, (d, wanted) in enumerate(targets):
                @pl.when(jnp.logical_and(wanted, d != me))
                def _(u=u, o=o, i=i, tile=tile, d=d):
                    final(u, o, i, tile, d).wait_send()

    @pl.when(jnp.logical_not(is_last))
    def _():
        to_last.wait_send()

    @pl.when(jnp.logical_and(core == 0, jnp.logical_not(is_zero)))
    def _():
        to_zero.wait_send()


def comm_scratch():
    dma = pltpu.SemaphoreType.DMA
    return [
        pltpu.VMEM((32, C), F32),
        pltpu.VMEM((8, 144, 128), BF),
        pltpu.VMEM((7, 144, 128), BF),
        pltpu.VMEM((440, 128), F32),
        pltpu.VMEM((6, 256, C), BF),
        pltpu.VMEM((16, 256, C), BF),
        pltpu.VMEM((16, 256, C), BF),
        pltpu.VMEM((16, 3, 64, C), BF),
        pltpu.VMEM((16, 64, C), BF),
        pltpu.VMEM((16, 3, 16, C), BF),
        pltpu.VMEM((16, 4, 16, 128), BF),
        pltpu.VMEM((16, 3, 16, 128), BF),
        pltpu.VMEM((16, 16, 128), F32),
        pltpu.VMEM((24, 16, 128), F32),
        pltpu.VMEM((392, 128), F32),
        pltpu.VMEM((16, C), F32),
        pltpu.VMEM((4, 16, 128), F32),
        pltpu.VMEM((3, 16, 128), F32),
        pltpu.VMEM((16, 128), F32),
        pltpu.VMEM((128, 16, 128), F32),
        pltpu.VMEM((64, 16, 128), F32),
        pltpu.VMEM((4, 32, 128), F32),
        dma((7,)), dma((7,)),
        dma((16,)), dma((16,)), dma((16,)), dma((16,)), dma((16,)), dma((16,)), dma((16,)), dma((16,)),
        dma((16, 2)), dma((6,)),
        dma((4,)), dma((4,)), dma((2,)), dma((2,)),
    ]


def encoder_call(packed, bal, cot, w1, w3, w2, bias, gain, shift):
    vm = pl.BlockSpec(memory_space=pltpu.VMEM)
    sm = pl.BlockSpec(memory_space=pltpu.SMEM)
    hb = pl.BlockSpec(memory_space=pl.ANY)
    return pl.pallas_call(
        encoder_kernel,
        out_shape=jax.ShapeDtypeStruct((264, 128), F32),
        in_specs=[vm, sm, vm, vm, hb, hb, vm, vm, vm],
        out_specs=vm,
        scratch_shapes=body_scratch() + comm_scratch(),
        compiler_params=pltpu.CompilerParams(
            vmem_limit_bytes=64 * 1024 * 1024 - 1024 * 64, collective_id=0, has_side_effects=True
        ),
    )(packed, bal, cot, w1, w3, w2, bias, gain, shift)


def pack_waves(x0, counts):
    frames = counts
    for k, st in ((10, 5), (3, 2), (3, 2), (3, 2), (3, 2), (2, 2), (2, 2)):
        frames = jnp.maximum((frames - k) // st + 1, 0)
    r = jnp.pad(x0.reshape(2, 400, 40), ((0, 0), (0, 32), (0, 0)))
    r = r.reshape(2, 3, 144, 40).transpose(0, 2, 1, 3).reshape(2, 144, 120)
    f = jnp.broadcast_to(frames.astype(BF)[:, None, None], (2, 144, 8))
    return jnp.concatenate([r, f], axis=2)


def normalize_wave(waveforms, lengths):
    positions = jnp.arange(waveforms.shape[1], dtype=jnp.int32)
    valid = (positions[None, :] < lengths[:, None]).astype(F32)
    divisor = jnp.maximum(lengths, 1).astype(F32)
    average = jnp.sum(waveforms * valid, axis=1) / divisor
    centred = (waveforms - average[:, None]) * valid
    spread = jnp.sum(centred * centred, axis=1) / divisor
    return (centred * lax.rsqrt(spread + 1e-07)[:, None]).astype(BF)


def on_device(waveforms, valid_counts, balance_list, cotangent, w_first, w_three, w_two, conv_bias, norm_gain, norm_shift):
    packed = pack_waves(normalize_wave(waveforms, valid_counts), valid_counts)
    shard = encoder_call(
        packed, balance_list, cotangent, w_first,
        w_three.reshape(4, 3 * C, C), w_two.reshape(2, 2 * C, C), conv_bias, norm_gain, norm_shift,
    )
    return shard.reshape(-1)[:SHARD]


def solution(mesh):
    both = ("dp", "narrow")
    in_specs = (
        P(both, None), P(both), P(both), P(both, None, None),
        P(), P(), P(), P(), P(), P(),
    )
    return jax.shard_map(on_device, mesh=mesh, in_specs=in_specs, out_specs=P(both), check_vma=False)
```

```python
import jax
import jax.numpy as jnp
from jax import lax
from jax.experimental import pallas as pl
from jax.experimental.pallas import tpu as pltpu
from jax.sharding import PartitionSpec as P

C = 512
F7 = 49
BF = jnp.bfloat16
F32 = jnp.float32

taps = (None, 3, 3, 3, 3, 2, 2)
phases = (8, 4, 2, 1, 1, 1, 1)
rows_of = (400, 400, 400, 400, 208, 112, 64)
in_blocks = (None, 9, 5, 3, 3, 2, 2)
ROW_TILE = {400: 400, 208: 208, 112: 112, 64: 64}


def dot(a, b):
    return jnp.dot(a, b, preferred_element_type=F32)


def dot_bt(a, b):
    return lax.dot_general(a, b, (((1,), (1,)), ((), ())), preferred_element_type=F32)


def dot_at(a, b):
    return lax.dot_general(a, b, (((0,), (0,)), ((), ())), preferred_element_type=F32)


HALF_ROOT = 0.7071067811865476
LOG2E = 1.4426950408889634
LOG2_C = -0.3257480647361593


def gelu_pair(m):
    phi = HALF_ROOT + HALF_ROOT * lax.erf(m)
    e = jnp.exp2(LOG2_C - (m * m) * LOG2E)
    return m * phi, phi + m * e


def loop_rows(rows, body, init):
    tile = ROW_TILE[rows]

    def step(i, carry):
        return body(pl.ds(pl.multiple_of(i * tile, tile), tile), carry)

    return lax.fori_loop(0, rows // tile, step, init)


def fold8(v):
    total = v[0:8]
    for i in range(8, v.shape[0], 8):
        total = total + v[i : i + 8]
    return total


def encoder_body(
    route, cot, w1, w3_hbm, w2_hbm, bias, gain, shift,
    emit, between, small,
    a0, w3, w2, wb, gw, x_refs, dg_refs, xh_refs, rs_refs, zs, zt, fs, f4, dz, gn, acc, bb, mm, bandf, wsem,
):
    w_copies = []
    for i in range(4):
        w_copies.append(pltpu.make_async_copy(w3_hbm.at[i], w3.at[i], wsem.at[i]))
    for i in range(2):
        w_copies.append(pltpu.make_async_copy(w2_hbm.at[i], w2.at[i], wsem.at[4 + i]))
    for c in w_copies:
        c.start()

    def weight(l, k):
        if l < 5:
            return w3[l - 1, k * C : (k + 1) * C, :]
        return w2[l - 5, k * C : (k + 1) * C, :]

    wf = w1[...].astype(F32)
    wc = wf - jnp.mean(wf, axis=-1, keepdims=True)
    b0 = bias[0:1, :]
    bc = b0 - jnp.mean(b0, axis=-1, keepdims=True)
    g0 = gain[0:1, :] * HALF_ROOT

    def split(v):
        hi = v.astype(BF).astype(F32)
        return hi, v - hi

    wc_hi, wc_lo = split(wc)
    bc_hi, bc_r = split(bc)
    bc_mid, bc_lo = split(bc_r)
    gw_hi, gw_lo = split(wc * g0)
    gb_hi, gb_lo = split(bc * g0)
    g_hi, g_lo = split(g0)
    for p in range(8):
        bandf[...] = jnp.zeros_like(bandf)
        bandf[5 * p : 5 * p + 10, :] = wc_hi
        bandf[45 + 5 * p : 55 + 5 * p, :] = wc_lo
        bandf[90:91, :] = bc_hi
        bandf[91:92, :] = bc_mid
        bandf[92:93, :] = bc_lo
        wb[:, p * C : (p + 1) * C] = bandf[...].astype(BF)
        bandf[5 * p : 5 * p + 10, :] = gw_hi
        bandf[45 + 5 * p : 55 + 5 * p, :] = gw_lo
        bandf[90:91, :] = gb_hi
        bandf[91:92, :] = gb_lo
        bandf[92:93, :] = jnp.zeros_like(bc_lo)
        bandf[126:127, :] = g_hi
        bandf[127:128, :] = g_lo
        gw[:, p * C : (p + 1) * C] = bandf[...].astype(BF)

    fs[400:424, :] = jnp.zeros((24, C), F32)
    f4[:, 400:424, :] = jnp.zeros((4, 24, 128), F32)

    last_frames = route()

    def activate(l, p, centred, zs):
        rows = rows_of[l]
        lanes = slice(p * C, (p + 1) * C)
        b = bias[l : l + 1, :]
        g = gain[l : l + 1, :] * HALF_ROOT
        s = shift[l : l + 1, :] * HALF_ROOT

        def body(r, carry):
            z = zs[r, :]
            if not centred:
                z = z + b
                z = z - jnp.sum(z, axis=-1, keepdims=True) * (1.0 / C)
            var = jnp.sum(z * z, axis=-1, keepdims=True) * (1.0 / C)
            rstd = lax.rsqrt(var + 1e-05)
            xh = z * rstd
            x, d = gelu_pair(xh * g + s)
            dg_refs[l][r, lanes] = d.astype(BF)
            if l > 0:
                xh_refs[l][r, lanes] = xh.astype(BF)
            rs_refs[l][p, r, :] = jnp.broadcast_to(rstd, (rstd.shape[0], 128))
            if l < 3:
                x_refs[l + 1][r, lanes] = x.astype(BF)
            if l < 3 and p == 0:
                fs[r, :] = x
            elif l < 6:
                for c in range(4):
                    f4[c, r, :] = x[:, c * 128 : (c + 1) * 128]
            return carry

        loop_rows(rows, body, 0)
        if l < 3 and p == 0:
            n = phases[l]
            x_refs[l + 1][:, n * C : (n + 1) * C] = fs[pl.ds(1, 400), :].astype(BF)

    for p in range(8):
        zt[p % 4] = dot(a0[...], wb[:, p * C : (p + 1) * C])
        activate(0, p, True, zt.at[p % 4])

    for l in range(1, 7):
        w_copies[l - 1].wait()
        k, rows = taps[l], rows_of[l]
        for p in range(phases[l]):
            w = w3[l - 1] if l < 5 else w2[l - 5]
            zt[p, 0:rows, :] = dot(x_refs[l][:, p * 2 * C : (p * 2 + k) * C], w)
            activate(l, p, False, zt.at[p])
        if 3 <= l < 6:
            n = rows_of[l + 1]
            for j in range(taps[l + 1]):
                for c in range(4):
                    x_refs[l + 1][:, j * C + c * 128 : j * C + (c + 1) * 128] = f4[
                        c, pl.ds(j, n, stride=2), :
                    ].astype(BF)

    row_id = lax.broadcasted_iota(jnp.int32, (F7, C), 0).astype(F32)
    zs[0:64, :] = jnp.zeros((64, C), F32)
    zs[0:F7, :] = jnp.where(row_id < last_frames, cot[0].astype(F32), 0.0)

    def got(src, r):
        if src is None:
            return jnp.concatenate([f4[c, r, :] for c in range(4)], axis=-1)
        return src[r, :]

    def norm_back(l, p, src, sums):
        lanes = slice(p * C, (p + 1) * C)
        out = slice((p + 1) * C, (p + 2) * C)
        g = gain[l : l + 1, :] * HALF_ROOT

        def body(r, carry):
            db, dga, dsh = carry
            gv = got(src, r) * dg_refs[l][r, lanes].astype(F32)
            xh = xh_refs[l][r, lanes].astype(F32)
            rstd = rs_refs[l][p, r, :][:, 0:1]
            dsh = dsh + fold8(gv)
            dga = dga + fold8(gv * xh)
            gx = gv * g
            m1 = jnp.sum(gx, axis=-1, keepdims=True) * (1.0 / C)
            m2 = jnp.sum(gx * xh, axis=-1, keepdims=True) * (1.0 / C)
            d = (gx - m1 - xh * m2) * rstd
            db = db + fold8(d)
            dz[r, out] = d.astype(BF)
            return db, dga, dsh

        return loop_rows(rows_of[l], body, sums)

    zero8 = jnp.zeros((8, C), F32)
    sums = norm_back(6, 0, zs, (zero8, zero8, zero8))

    def store_sums(l, sums):
        for j in range(3):
            total = jnp.sum(sums[j], axis=0, keepdims=True)
            small[10 + 7 * j + l : 11 + 7 * j + l, :] = total if j == 0 else total * HALF_ROOT

    for l in range(6, 0, -1):
        k, rows, n = taps[l], rows_of[l], phases[l]
        store_sums(l, sums)
        if k == 3:
            fs[8 : 8 + rows, :] = dz[0:rows, n * C : (n + 1) * C].astype(F32)
            fs[0:8, :] = jnp.zeros((8, C), F32)
            dz[0:rows, 0:C] = fs[pl.ds(7, rows), :].astype(BF)

        for j in range(k):
            for p in range(n):
                part = dot_at(
                    x_refs[l][:, (2 * p + j) * C : (2 * p + j + 1) * C], dz[0:rows, (p + 1) * C : (p + 2) * C]
                )
                if p == 0:
                    acc[j * C : (j + 1) * C, :] = part
                else:
                    acc[j * C : (j + 1) * C, :] += part
            emit(l, j, acc)
        between("wgrad", l, 0)

        if l > 3:
            here = dz[0:rows, C : 2 * C]
            even = dot_bt(here, weight(l, 0))
            if k == 3:
                even = even + dot_bt(dz[0:rows, 0:C], weight(l, 2))
            odd = dot_bt(here, weight(l, 1))
            half = rows_of[l - 1] // 2
            for c in range(4):
                f4[c, pl.ds(0, half, stride=2), :] = even[:half, c * 128 : (c + 1) * 128]
                f4[c, pl.ds(1, half, stride=2), :] = odd[:half, c * 128 : (c + 1) * 128]
            sums = norm_back(l - 1, 0, None, (zero8, zero8, zero8))
            between("back", l - 1, 0)
        elif l > 1:
            def dgrad(p, carry, l=l):
                here = dz[:, pl.ds(pl.multiple_of((p + 1) * C, C), C)]
                before = dz[:, pl.ds(pl.multiple_of(p * C, C), C)]
                zt[2 * p] = dot_bt(here, weight(l, 0)) + dot_bt(before, weight(l, 2))
                zt[2 * p + 1] = dot_bt(here, weight(l, 1))
                return carry

            for p in range(n):
                dgrad(p, 0)

            def back(p, carry, l=l):
                return norm_back(l - 1, p, zt.at[p], carry)

            sums = (zero8, zero8, zero8)
            for p in range(2 * n):
                sums = back(p, sums)
                between("back", l - 1, p)
        else:
            lane = lax.broadcasted_iota(jnp.int32, (400, 128), 1)

            def one(q, src, dsh):
                lanes = slice(q * C, (q + 1) * C)
                zq, gq = zt.at[q % 4], gn.at[q % 2]
                zq[...] = src

                def body(r, dsh):
                    gv = zq[r, :] * dg_refs[0][r, lanes].astype(F32)
                    gq[r, 0:C] = (gv * rs_refs[0][q, r, :][:, 0:1]).astype(BF)
                    return dsh + fold8(gv)

                dsh = loop_rows(400, body, dsh)
                u = dot_bt(gq[:, 0:C], gw[:, lanes])
                a = a0[...].astype(F32)
                m2 = jnp.sum(a * u, axis=-1, keepdims=True) * (1.0 / C)
                m1 = jnp.sum(jnp.where(lane >= 126, u, 0.0), axis=-1, keepdims=True) * (1.0 / C)
                rstd = rs_refs[0][q]
                rhs = jnp.where(lane == 127, m1, a * (rstd * rstd * m2))
                hi = rhs.astype(BF)
                gq[:, C : C + 128] = hi
                gq[:, C + 128 : C + 256] = (rhs - hi.astype(F32)).astype(BF)
                both = dot_at(a0[...], gq[...])
                bb[q * 128 : (q + 1) * 128, :] = both[:, 0:C]
                mm[q] = both[:, C : C + 128] + both[:, C + 128 : C + 256]
                return dsh

            dsh = zero8
            for p in range(4):
                here = dz[:, (p + 1) * C : (p + 2) * C]
                before = dz[:, p * C : (p + 1) * C]
                dsh = one(2 * p, dot_bt(here, weight(1, 0)) + dot_bt(before, weight(1, 2)), dsh)
                dsh = one(2 * p + 1, dot_bt(here, weight(1, 1)), dsh)
                between("first", 0, p)
            dw = jnp.zeros((10, C), F32)
            db = jnp.zeros((1, C), F32)
            dga = jnp.zeros((1, C), F32)
            for q in range(8):
                bq = bb[q * 128 : (q + 1) * 128, :]
                band = wb[:, q * C : (q + 1) * C].astype(F32)
                dga = dga + jnp.sum(bq * band, axis=0, keepdims=True)
                m = mm[q]
                bandf[...] = bq * g0 - m[:, 127:128] - jnp.dot(
                    m, band, preferred_element_type=F32, precision=lax.Precision.HIGHEST
                )
                dw = dw + bandf[5 * q : 5 * q + 10, :]
                db = db + bandf[90:91, :]
            small[0:10, :] = dw
            small[10:11, :] = db
            small[17:18, :] = dga * HALF_ROOT
            small[24:25, :] = jnp.sum(dsh, axis=0, keepdims=True) * HALF_ROOT
            small[31:32, :] = jnp.zeros((1, C), F32)


def body_scratch():
    s = [
        pltpu.VMEM((400, 128), BF),
        pltpu.VMEM((4, 3 * C, C), BF),
        pltpu.VMEM((2, 2 * C, C), BF),
        pltpu.VMEM((128, 8 * C), BF),
        pltpu.VMEM((128, 8 * C), BF),
    ]
    s.append([pltpu.VMEM((rows_of[l], in_blocks[l] * C), BF) for l in range(1, 7)])
    s.append([pltpu.VMEM((rows_of[l], phases[l] * C), BF) for l in range(7)])
    s.append([pltpu.VMEM((rows_of[l], phases[l] * C), BF) for l in range(1, 7)])
    s.append([pltpu.VMEM((phases[l], rows_of[l], 128), F32) for l in range(7)])
    s += [
        pltpu.VMEM((400, C), F32),
        pltpu.VMEM((4, 400, C), F32),
        pltpu.VMEM((424, C), F32),
        pltpu.VMEM((4, 424, 128), F32),
        pltpu.VMEM((400, 5 * C), BF),
        pltpu.VMEM((2, 400, C + 256), BF),
        pltpu.VMEM((3 * C, C), F32),
        pltpu.VMEM((8, 128, 128), F32),
        pltpu.VMEM((128, C), F32),
        pltpu.SemaphoreType.DMA((6,)),
    ]
    return s


MESH = pl.DeviceIdType.MESH
SHARD = 32892
ORDERS = (("x", "y", "z"), ("y", "z", "x"), ("z", "x", "y"))


def unit_of(l, k):
    return (l - 1) * 3 + k if l < 5 else 12 + (l - 5) * 2 + k


def order_of(l, k):
    return ORDERS[(k + (2 if l == 6 else 0)) % 3]


def first_tile(d):
    return lax.div(SHARD * d + 3072, 8192) - 1


def encoder_kernel(
    packed, cnt, bal, cot, w1, w3_hbm, w2_hbm, bias, gain, shift, out, *scratch
):
    (a0, w3, w2, wb, gw, xs, dgs, xhs, rss, zs, zt, fs, f4, dz, gn, acc, mm, bandf, wsem,
     small, pk, sb, rb, xr, s0, keep, r0, r1, h2, r2, h3, r3, tl, own, fl, rs0, hs, rs1, ts, root, root0, sm4,
     sb_sem, rb_sem, s0_sem, r0_sem, s1_sem, r1_sem, s2_sem, r2_sem, s3_sem, r3_sem, t_sem, own_sem,
     q_send, q_recv, root_sem, qr_send) = scratch

    dp = lax.axis_index("dp")
    nw = lax.axis_index("narrow")
    z, y = lax.div(dp, 4), lax.rem(dp, 4)
    x, core = lax.div(nw, 2), lax.rem(nw, 2)
    me = dp * 8 + nw
    at = {"x": x, "y": y, "z": z}

    def peer(axis, delta):
        if axis == "core":
            return (dp, x * 2 + (1 - core))
        if axis == "x":
            return (dp, lax.rem(x + delta, 4) * 2 + core)
        if axis == "y":
            return (z * 4 + lax.rem(y + delta, 4), nw)
        return (lax.rem(z + delta, 4) * 4 + y, nw)

    def remote(src, dst, send, recv, device):
        return pltpu.make_async_remote_copy(
            src_ref=src, dst_ref=dst, send_sem=send, recv_sem=recv, device_id=device, device_id_type=MESH
        )

    barrier = pltpu.get_barrier_semaphore()
    for d in range(1, 8):
        pl.semaphore_signal(barrier, inc=1, device_id=(dp, lax.rem(nw + d, 8)), device_id_type=MESH)
    for axis in ("y", "z"):
        for d in range(1, 4):
            pl.semaphore_signal(barrier, inc=1, device_id=peer(axis, d), device_id_type=MESH)

    def normalise(s):
        n = cnt[s]
        row = lax.broadcasted_iota(jnp.int32, (144, 128), 0)
        lane = lax.broadcasted_iota(jnp.int32, (144, 128), 1)
        block = jnp.where(lane >= 40, 1, 0) + jnp.where(lane >= 80, 1, 0)
        row = row + block * 144
        place = row * 40 + lane - block * 40
        valid = (row < 400) & (lane < 120) & (place < n)
        w = jnp.where(valid, packed[s], 0.0)
        over = jnp.full((1, 1), jnp.maximum(n, 1), jnp.int32).astype(F32)
        total = jnp.sum(jnp.sum(w, axis=0, keepdims=True), axis=1, keepdims=True)
        centred = jnp.where(valid, w - total / over, 0.0)
        square = jnp.sum(jnp.sum(centred * centred, axis=0, keepdims=True), axis=1, keepdims=True)
        value = centred * lax.rsqrt(square / over + 1e-07)
        frames = n
        for k, st in ((10, 5), (3, 2), (3, 2), (3, 2), (3, 2), (2, 2), (2, 2)):
            frames = jnp.maximum(lax.div(frames - k + st, st), 0)
        return jnp.where(lane >= 120, jnp.full((144, 128), frames, jnp.int32).astype(F32), value).astype(BF)

    for s in range(2):
        pk[s] = normalise(s)

    def send_waves():
        for d in range(8):
            there = lax.rem(nw + d, 8)
            m0 = jnp.where(bal[0] == there, 1.0, 0.0)
            m1 = jnp.where(bal[1] == there, 1.0, 0.0)
            sb[d] = (pk[0].astype(F32) * m0 + pk[1].astype(F32) * m1).astype(BF)
        pl.semaphore_wait(barrier, 13)
        copies = []
        for d in range(1, 8):
            c = remote(sb.at[d], rb.at[d - 1], sb_sem.at[d - 1], rb_sem.at[d - 1], (dp, lax.rem(nw + d, 8)))
            c.start()
            copies.append(c)
        return copies

    def route():
        g = sb[0].astype(F32)
        for d in range(1, 8):
            copies[d - 1].wait()
            g = g + rb[d - 1].astype(F32)
        for b in range(3):
            xr[144 * b : 144 * b + 144, :] = g if b == 0 else pltpu.roll(g, 128 - 40 * b, 1)
        xr[432:440, :] = jnp.zeros((8, 128), F32)
        v0 = xr[0:400, :]
        v1 = pltpu.roll(xr[pl.ds(1, 400), :], 40, 1)
        lane = lax.broadcasted_iota(jnp.int32, (400, 128), 1)
        one = jnp.where(lane < 40, v0, jnp.where(lane < 45, v1, 0.0))
        ones = jnp.where((lane >= 90) & (lane < 93), 1.0, 0.0)
        a0[...] = (one + pltpu.roll(one, 45, 1) + ones).astype(BF)
        return g[0:1, 127:128]

    def units(l):
        return [(k, unit_of(l, k), order_of(l, k)) for k in range(taps[l])]

    def slot(l, k):
        return (l % 2) * 3 + k

    def copy0(l, k, u):
        return remote(s0.at[slot(l, k)], r0.at[u], s0_sem.at[u], r0_sem.at[u], peer("core", 1))

    def move0(l, k, acc):
        u, o = unit_of(l, k), order_of(l, k)
        if l + 2 <= 6 and k < taps[l + 2]:
            copy0(l + 2, k, unit_of(l + 2, k)).wait_send()

        def spread(ref, i, half):
            for xx in range(4):
                for yy in range(4):
                    rows = pl.ds(pl.multiple_of(half * 64 + (k * C + xx * 128 + yy * 16), 16), 16)
                    v = acc[rows, :].astype(BF)
                    for zz in range(4):
                        by = {"x": xx, "y": yy, "z": zz}
                        ref[i, by[o[0]], by[o[1]], by[o[2]]] = v[:, zz * 128 : (zz + 1) * 128]

        spread(s0, slot(l, k), 1 - core)
        copy0(l, k, u).start()
        spread(keep, u, core)

    def whole(ref, send, recv, o):
        return remote(ref, ref, send, recv, peer(o, 1))

    def hand_on(buf, got, u, axis, send, recv):
        for d in range(1, 4):
            j = lax.rem(at[axis] + d, 4)
            remote(buf.at[u, j], got.at[u, d - 1], send.at[u], recv.at[u], peer(axis, d)).start()

    def summed(buf, got, u, axis):
        v = buf[u, at[axis]].astype(F32)
        for d in range(3):
            v = v + got[u, d].astype(F32)
        return v.astype(BF)

    def chosen(l, only):
        return [t for t in units(l) if t[0] in only]

    def move1(l, only):
        for k, u, o in chosen(l, only):
            copy0(l, k, u).wait_recv()
            for j in range(4):
                keep[u, j] = (keep[u, j].astype(F32) + r0[u, j].astype(F32)).astype(BF)
            hand_on(keep, r1, u, o[0], s1_sem, r1_sem)

    def move2(l, only):
        for k, u, o in chosen(l, only):
            whole(r1.at[u], s1_sem.at[u], r1_sem.at[u], o[0]).wait_recv()
            h2[u] = summed(keep, r1, u, o[0])
            hand_on(h2, r2, u, o[1], s2_sem, r2_sem)

    def move3(l, only):
        for k, u, o in chosen(l, only):
            whole(r2.at[u], s2_sem.at[u], r2_sem.at[u], o[1]).wait_recv()
            h3[u] = summed(h2, r2, u, o[1])
            hand_on(h3, r3, u, o[2], s3_sem, r3_sem)

    def owners(u):
        tile = u * 32 + x * 8 + core * 4 + y
        start = (10 + 16 * tile) * C
        first = lax.div(start, SHARD)
        last = lax.div(start + 8191, SHARD)
        return tile, ((first, True), (last, last != first))

    def final(u, i, tile, d):
        s = tile - first_tile(d)
        device = (lax.div(d, 8), lax.rem(d, 8))
        return remote(tl.at[u], own.at[s, z], t_sem.at[u, i], own_sem.at[s], device)

    def final_here(u, tile, d):
        return pltpu.make_async_copy(tl.at[u], own.at[tile - first_tile(d), z], own_sem.at[tile - first_tile(d)])

    def move4(l, only):
        for k, u, o in chosen(l, only):
            whole(r3.at[u], s3_sem.at[u], r3_sem.at[u], o[2]).wait_recv()
            tl[u] = summed(h3, r3, u, o[2])
            tile, targets = owners(u)
            for i, (d, wanted) in enumerate(targets):
                @pl.when(jnp.logical_and(wanted, d != me))
                def _(u=u, i=i, tile=tile, d=d):
                    final(u, i, tile, d).start()

                @pl.when(jnp.logical_and(wanted, d == me))
                def _(u=u, tile=tile, d=d):
                    final_here(u, tile, d).start()

    def emit(l, k, acc):
        move0(l, k, acc)

    plan = {
        ("wgrad", 4, 0): [(move1, 6)],
        ("wgrad", 3, 0): [(move1, 5)],
        ("back", 2, 1): [(move1, 4)],
        ("wgrad", 2, 0): [(move2, 6)],
        ("back", 1, 0): [(move1, 3), (move2, 5)],
        ("back", 1, 2): [(move3, 6), (move2, 4)],
        ("back", 1, 3): [(move1, 2), (move3, 5)],
        ("wgrad", 1, 0): [(move2, 3), (move3, 4), (move4, 6), (move4, 5), (move1, 1, (0,))],
        ("first", 0, 0): [(move1, 1, (1, 2)), (move4, 4)],
        ("first", 0, 1): [(move2, 2), (move3, 3)],
        ("first", 0, 2): [(move4, 3)],
        ("first", 0, 3): [(move3, 2), (move2, 1)],
    }

    def between(kind, l, p):
        for move, layer, *only in plan.get((kind, l, p), ()):
            move(layer, only[0] if only else (0, 1, 2))

    fl[...] = jnp.zeros_like(fl)
    copies = send_waves()
    encoder_body(
        route, cot, w1, w3_hbm, w2_hbm, bias, gain, shift, emit, between, small,
        a0, w3, w2, wb, gw, [None] + list(xs), list(dgs), [None] + list(xhs), list(rss),
        zs, zt, fs, f4, dz, gn, acc, acc, mm, bandf, wsem,
    )

    def rows_of_core(c):
        return pl.ds(pl.multiple_of(c * 16, 16), 16)

    c0 = remote(small.at[rows_of_core(1 - core)], rs0, q_send.at[0], q_recv.at[0], peer("core", 1))
    c0.start()
    move4(2, (0, 1, 2))
    c0.wait()
    v = small[rows_of_core(core), :] + rs0[...]
    for c in range(4):
        hs[c] = v[:, c * 128 : (c + 1) * 128]
    cx = []
    for d in range(1, 4):
        c1 = remote(hs.at[lax.rem(x + d, 4)], rs1.at[d - 1], q_send.at[d], q_recv.at[d], peer("x", d))
        c1.start()
        cx.append(c1)
    move3(1, (0, 1, 2))
    v = hs[x]
    for d in range(3):
        cx[d].wait()
        v = v + rs1[d]
    ts[...] = v
    to_last = remote(ts, root.at[me], qr_send.at[0], root_sem.at[0], (15, 7))
    my_last = pltpu.make_async_copy(ts, root.at[me], root_sem.at[0])
    to_zero = remote(ts, root0.at[dp * 4 + x], qr_send.at[1], root_sem.at[1], (0, 0))
    my_zero = pltpu.make_async_copy(ts, root0.at[dp * 4 + x], root_sem.at[1])
    is_last = me == 127
    is_zero = me == 0

    @pl.when(jnp.logical_not(is_last))
    def _():
        to_last.start()

    @pl.when(is_last)
    def _():
        my_last.start()

    @pl.when(jnp.logical_and(core == 0, jnp.logical_not(is_zero)))
    def _():
        to_zero.start()

    @pl.when(is_zero)
    def _():
        my_zero.start()

    move4(1, (0, 1, 2))

    low = first_tile(me)
    high = jnp.minimum(lax.div(SHARD * me + SHARD - 1 + 3072, 8192) - 1, 511)

    for s in range(6):
        @pl.when(jnp.logical_and(low + s >= 0, low + s <= high))
        def _(s=s):
            pltpu.make_async_copy(own.at[s], own.at[s], own_sem.at[s]).wait()
            for c in range(4):
                fl[pl.ds(64 * s + c, 16, stride=4), :] = own[s, c].astype(F32)

    @pl.when(is_last)
    def _():
        pltpu.make_async_copy(root, root, root_sem.at[0]).wait()
        for c in range(4):
            for h in range(2):
                v = root[2 * c + h]
                for i in range(1, 16):
                    v = v + root[8 * i + 2 * c + h]
                sm4[c, 16 * h : 16 * h + 16, :] = v
            fl[pl.ds(192 + c, 21, stride=4), :] = sm4[c, 10:31, :]

    @pl.when(is_zero)
    def _():
        pltpu.make_async_copy(root0, root0, root_sem.at[1]).wait()
        for c in range(4):
            v = root0[c]
            for i in range(1, 16):
                v = v + root0[4 * i + c]
            sm4[c, 0:16, :] = v
            fl[pl.ds(24 + c, 10, stride=4), :] = sm4[c, 0:10, :]

    offset = SHARD * me - C * (10 + 16 * low)
    row = lax.div(offset, 128)
    turn = lax.rem(offset, 128)
    back = lax.rem(128 - turn, 128)
    upper = pltpu.roll(fl[pl.ds(row, 264), :], back, 1)
    lower = pltpu.roll(fl[pl.ds(row + 1, 264), :], back, 1)
    lane = lax.broadcasted_iota(jnp.int32, (264, 128), 1)
    out[...] = jnp.where(lane < 128 - turn, upper, lower)

    for l in range(1, 7):
        for k, u, o in units(l):
            if l <= 2:
                copy0(l, k, u).wait_send()
            elif k >= taps[l - 2]:
                copy0(l, k, u).wait_send()
            whole(r1.at[u], s1_sem.at[u], r1_sem.at[u], o[0]).wait_send()
            whole(r2.at[u], s2_sem.at[u], r2_sem.at[u], o[1]).wait_send()
            whole(r3.at[u], s3_sem.at[u], r3_sem.at[u], o[2]).wait_send()
            tile, targets = owners(u)
            for i, (d, wanted) in enumerate(targets):
                @pl.when(jnp.logical_and(wanted, d != me))
                def _(u=u, i=i, tile=tile, d=d):
                    final(u, i, tile, d).wait_send()

    @pl.when(jnp.logical_not(is_last))
    def _():
        to_last.wait_send()

    @pl.when(jnp.logical_and(core == 0, jnp.logical_not(is_zero)))
    def _():
        to_zero.wait_send()


def comm_scratch():
    dma = pltpu.SemaphoreType.DMA
    return [
        pltpu.VMEM((32, C), F32),
        pltpu.VMEM((2, 144, 128), BF),
        pltpu.VMEM((8, 144, 128), BF),
        pltpu.VMEM((7, 144, 128), BF),
        pltpu.VMEM((440, 128), F32),
        pltpu.VMEM((6, 4, 4, 4, 16, 128), BF),
        pltpu.VMEM((16, 4, 4, 4, 16, 128), BF),
        pltpu.VMEM((16, 4, 4, 4, 16, 128), BF),
        pltpu.VMEM((16, 3, 4, 4, 16, 128), BF),
        pltpu.VMEM((16, 4, 4, 16, 128), BF),
        pltpu.VMEM((16, 3, 4, 16, 128), BF),
        pltpu.VMEM((16, 4, 16, 128), BF),
        pltpu.VMEM((16, 3, 16, 128), BF),
        pltpu.VMEM((16, 16, 128), BF),
        pltpu.VMEM((6, 4, 16, 128), BF),
        pltpu.VMEM((392, 128), F32),
        pltpu.VMEM((16, C), F32),
        pltpu.VMEM((4, 16, 128), F32),
        pltpu.VMEM((3, 16, 128), F32),
        pltpu.VMEM((16, 128), F32),
        pltpu.VMEM((128, 16, 128), F32),
        pltpu.VMEM((64, 16, 128), F32),
        pltpu.VMEM((4, 32, 128), F32),
        dma((7,)), dma((7,)),
        dma((16,)), dma((16,)), dma((16,)), dma((16,)), dma((16,)), dma((16,)), dma((16,)), dma((16,)),
        dma((16, 2)), dma((6,)),
        dma((4,)), dma((4,)), dma((2,)), dma((2,)),
    ]


def encoder_call(packed, cnt, bal, cot, w1, w3, w2, bias, gain, shift):
    vm = pl.BlockSpec(memory_space=pltpu.VMEM)
    sm = pl.BlockSpec(memory_space=pltpu.SMEM)
    hb = pl.BlockSpec(memory_space=pl.ANY)
    return pl.pallas_call(
        encoder_kernel,
        out_shape=jax.ShapeDtypeStruct((264, 128), F32),
        in_specs=[vm, sm, sm, vm, vm, hb, hb, vm, vm, vm],
        out_specs=vm,
        scratch_shapes=body_scratch() + comm_scratch(),
        compiler_params=pltpu.CompilerParams(
            vmem_limit_bytes=64 * 1024 * 1024 - 1024 * 64, collective_id=0, has_side_effects=True
        ),
    )(packed, cnt, bal, cot, w1, w3, w2, bias, gain, shift)


def pack_waves(waves):
    r = jnp.pad(waves.reshape(2, 400, 40), ((0, 0), (0, 32), (0, 0)))
    r = r.reshape(2, 3, 144, 40).transpose(0, 2, 1, 3).reshape(2, 144, 120)
    return jnp.pad(r, ((0, 0), (0, 0), (0, 8)))


def on_device(waveforms, valid_counts, balance_list, cotangent, w_first, w_three, w_two, conv_bias, norm_gain, norm_shift):
    shard = encoder_call(
        pack_waves(waveforms), valid_counts, balance_list, cotangent, w_first,
        w_three.reshape(4, 3 * C, C), w_two.reshape(2, 2 * C, C), conv_bias, norm_gain, norm_shift,
    )
    return shard.reshape(-1)[:SHARD]


def solution(mesh):
    both = ("dp", "narrow")
    in_specs = (
        P(both, None), P(both), P(both), P(both, None, None),
        P(), P(), P(), P(), P(), P(),
    )
    return jax.shard_map(on_device, mesh=mesh, in_specs=in_specs, out_specs=P(both), check_vma=False)
```

```python
import jax
import jax.numpy as jnp
from jax import lax
from jax.experimental import pallas as pl
from jax.experimental.pallas import tpu as pltpu
from jax.sharding import PartitionSpec as P

C = 512
F7 = 49
BF = jnp.bfloat16
F32 = jnp.float32

taps = (None, 3, 3, 3, 3, 2, 2)
phases = (8, 4, 2, 1, 1, 1, 1)
rows_of = (400, 400, 400, 400, 208, 112, 64)
in_blocks = (None, 9, 5, 3, 3, 2, 2)
ROW_TILE = {400: 400, 208: 208, 112: 112, 64: 64}


def dot(a, b):
    return jnp.dot(a, b, preferred_element_type=F32)


def dot_bt(a, b):
    return lax.dot_general(a, b, (((1,), (1,)), ((), ())), preferred_element_type=F32)


def dot_at(a, b):
    return lax.dot_general(a, b, (((0,), (0,)), ((), ())), preferred_element_type=F32)


HALF_ROOT = 0.7071067811865476
LOG2E = 1.4426950408889634
LOG2_C = -0.3257480647361593


def gelu_pair(m):
    phi = HALF_ROOT + HALF_ROOT * lax.erf(m)
    e = jnp.exp2(LOG2_C - (m * m) * LOG2E)
    return m * phi, phi + m * e


def loop_rows(rows, body, init):
    tile = ROW_TILE[rows]

    def step(i, carry):
        return body(pl.ds(pl.multiple_of(i * tile, tile), tile), carry)

    return lax.fori_loop(0, rows // tile, step, init)


def fold8(v):
    total = v[0:8]
    for i in range(8, v.shape[0], 8):
        total = total + v[i : i + 8]
    return total


def encoder_body(
    route, cot, w1, w3_hbm, w2_hbm, bias, gain, shift,
    emit, between, small,
    a0, w3, w2, wb, gw, x_refs, dg_refs, xh_refs, rs_refs, zs, zt, fs, f4, dz, gn, acc, bb, mm, bandf, wsem,
):
    w_copies = []
    for i in range(4):
        w_copies.append(pltpu.make_async_copy(w3_hbm.at[i], w3.at[i], wsem.at[i]))
    for i in range(2):
        w_copies.append(pltpu.make_async_copy(w2_hbm.at[i], w2.at[i], wsem.at[4 + i]))
    for c in w_copies:
        c.start()

    def weight(l, k):
        if l < 5:
            return w3[l - 1, k * C : (k + 1) * C, :]
        return w2[l - 5, k * C : (k + 1) * C, :]

    wf = w1[...].astype(F32)
    wc = wf - jnp.mean(wf, axis=-1, keepdims=True)
    b0 = bias[0:1, :]
    bc = b0 - jnp.mean(b0, axis=-1, keepdims=True)
    g0 = gain[0:1, :] * HALF_ROOT

    def split(v):
        hi = v.astype(BF).astype(F32)
        return hi, v - hi

    wc_hi, wc_lo = split(wc)
    bc_hi, bc_r = split(bc)
    bc_mid, bc_lo = split(bc_r)
    gw_hi, gw_lo = split(wc * g0)
    gb_hi, gb_lo = split(bc * g0)
    g_hi, g_lo = split(g0)
    for p in range(8):
        bandf[...] = jnp.zeros_like(bandf)
        bandf[5 * p : 5 * p + 10, :] = wc_hi
        bandf[45 + 5 * p : 55 + 5 * p, :] = wc_lo
        bandf[90:91, :] = bc_hi
        bandf[91:92, :] = bc_mid
        bandf[92:93, :] = bc_lo
        wb[:, p * C : (p + 1) * C] = bandf[...].astype(BF)
        bandf[5 * p : 5 * p + 10, :] = gw_hi
        bandf[45 + 5 * p : 55 + 5 * p, :] = gw_lo
        bandf[90:91, :] = gb_hi
        bandf[91:92, :] = gb_lo
        bandf[92:93, :] = jnp.zeros_like(bc_lo)
        bandf[126:127, :] = g_hi
        bandf[127:128, :] = g_lo
        gw[:, p * C : (p + 1) * C] = bandf[...].astype(BF)

    fs[400:424, :] = jnp.zeros((24, C), F32)
    f4[:, 400:424, :] = jnp.zeros((4, 24, 128), F32)

    last_frames = route()

    def activate(l, p, centred, zs):
        rows = rows_of[l]
        lanes = slice(p * C, (p + 1) * C)
        b = bias[l : l + 1, :]
        g = gain[l : l + 1, :] * HALF_ROOT
        s = shift[l : l + 1, :] * HALF_ROOT

        def body(r, carry):
            z = zs[r, :]
            if not centred:
                z = z + b
                z = z - jnp.sum(z, axis=-1, keepdims=True) * (1.0 / C)
            var = jnp.sum(z * z, axis=-1, keepdims=True) * (1.0 / C)
            rstd = lax.rsqrt(var + 1e-05)
            xh = z * rstd
            x, d = gelu_pair(xh * g + s)
            dg_refs[l][r, lanes] = d.astype(BF)
            if l > 0:
                xh_refs[l][r, lanes] = xh.astype(BF)
            rs_refs[l][p, r, :] = jnp.broadcast_to(rstd, (rstd.shape[0], 128))
            if l < 3:
                x_refs[l + 1][r, lanes] = x.astype(BF)
            if l < 3 and p == 0:
                fs[r, :] = x
            elif l < 6:
                for c in range(4):
                    f4[c, r, :] = x[:, c * 128 : (c + 1) * 128]
            return carry

        loop_rows(rows, body, 0)
        if l < 3 and p == 0:
            n = phases[l]
            x_refs[l + 1][:, n * C : (n + 1) * C] = fs[pl.ds(1, 400), :].astype(BF)

    for p in range(8):
        zt[p % 4] = dot(a0[...], wb[:, p * C : (p + 1) * C])
        activate(0, p, True, zt.at[p % 4])

    for l in range(1, 7):
        w_copies[l - 1].wait()
        k, rows = taps[l], rows_of[l]
        for p in range(phases[l]):
            w = w3[l - 1] if l < 5 else w2[l - 5]
            zt[p, 0:rows, :] = dot(x_refs[l][:, p * 2 * C : (p * 2 + k) * C], w)
            activate(l, p, False, zt.at[p])
        if 3 <= l < 6:
            n = rows_of[l + 1]
            for j in range(taps[l + 1]):
                for c in range(4):
                    x_refs[l + 1][:, j * C + c * 128 : j * C + (c + 1) * 128] = f4[
                        c, pl.ds(j, n, stride=2), :
                    ].astype(BF)

    row_id = lax.broadcasted_iota(jnp.int32, (F7, C), 0).astype(F32)
    zs[0:64, :] = jnp.zeros((64, C), F32)
    zs[0:F7, :] = jnp.where(row_id < last_frames, cot[0].astype(F32), 0.0)

    def got(src, r):
        if src is None:
            return jnp.concatenate([f4[c, r, :] for c in range(4)], axis=-1)
        return src[r, :]

    def norm_back(l, p, src, sums):
        lanes = slice(p * C, (p + 1) * C)
        out = slice((p + 1) * C, (p + 2) * C)
        g = gain[l : l + 1, :] * HALF_ROOT

        def body(r, carry):
            db, dga, dsh = carry
            gv = got(src, r) * dg_refs[l][r, lanes].astype(F32)
            xh = xh_refs[l][r, lanes].astype(F32)
            rstd = rs_refs[l][p, r, :][:, 0:1]
            dsh = dsh + fold8(gv)
            dga = dga + fold8(gv * xh)
            gx = gv * g
            m1 = jnp.sum(gx, axis=-1, keepdims=True) * (1.0 / C)
            m2 = jnp.sum(gx * xh, axis=-1, keepdims=True) * (1.0 / C)
            d = (gx - m1 - xh * m2) * rstd
            db = db + fold8(d)
            dz[r, out] = d.astype(BF)
            return db, dga, dsh

        return loop_rows(rows_of[l], body, sums)

    zero8 = jnp.zeros((8, C), F32)
    sums = norm_back(6, 0, zs, (zero8, zero8, zero8))

    def store_sums(l, sums):
        for j in range(3):
            total = jnp.sum(sums[j], axis=0, keepdims=True)
            small[10 + 7 * j + l : 11 + 7 * j + l, :] = total if j == 0 else total * HALF_ROOT

    for l in range(6, 0, -1):
        k, rows, n = taps[l], rows_of[l], phases[l]
        store_sums(l, sums)
        if k == 3:
            fs[8 : 8 + rows, :] = dz[0:rows, n * C : (n + 1) * C].astype(F32)
            fs[0:8, :] = jnp.zeros((8, C), F32)
            dz[0:rows, 0:C] = fs[pl.ds(7, rows), :].astype(BF)

        for j in range(k):
            for p in range(n):
                part = dot_at(
                    x_refs[l][:, (2 * p + j) * C : (2 * p + j + 1) * C], dz[0:rows, (p + 1) * C : (p + 2) * C]
                )
                if p == 0:
                    acc[j * C : (j + 1) * C, :] = part
                else:
                    acc[j * C : (j + 1) * C, :] += part
            emit(l, j, acc)
        between("wgrad", l, 0)

        if l > 3:
            here = dz[0:rows, C : 2 * C]
            even = dot_bt(here, weight(l, 0))
            if k == 3:
                even = even + dot_bt(dz[0:rows, 0:C], weight(l, 2))
            odd = dot_bt(here, weight(l, 1))
            half = rows_of[l - 1] // 2
            for c in range(4):
                f4[c, pl.ds(0, half, stride=2), :] = even[:half, c * 128 : (c + 1) * 128]
                f4[c, pl.ds(1, half, stride=2), :] = odd[:half, c * 128 : (c + 1) * 128]
            sums = norm_back(l - 1, 0, None, (zero8, zero8, zero8))
            between("back", l - 1, 0)
        elif l > 1:
            def dgrad(p, carry, l=l):
                here = dz[:, pl.ds(pl.multiple_of((p + 1) * C, C), C)]
                before = dz[:, pl.ds(pl.multiple_of(p * C, C), C)]
                zt[2 * p] = dot_bt(here, weight(l, 0)) + dot_bt(before, weight(l, 2))
                zt[2 * p + 1] = dot_bt(here, weight(l, 1))
                return carry

            for p in range(n):
                dgrad(p, 0)

            def back(p, carry, l=l):
                return norm_back(l - 1, p, zt.at[p], carry)

            sums = (zero8, zero8, zero8)
            for p in range(2 * n):
                sums = back(p, sums)
                between("back", l - 1, p)
        else:
            lane = lax.broadcasted_iota(jnp.int32, (400, 128), 1)

            def one(q, src, dsh):
                lanes = slice(q * C, (q + 1) * C)
                zq, gq = zt.at[q % 4], gn.at[q % 2]
                zq[...] = src

                def body(r, dsh):
                    gv = zq[r, :] * dg_refs[0][r, lanes].astype(F32)
                    gq[r, 0:C] = (gv * rs_refs[0][q, r, :][:, 0:1]).astype(BF)
                    return dsh + fold8(gv)

                dsh = loop_rows(400, body, dsh)
                u = dot_bt(gq[:, 0:C], gw[:, lanes])
                a = a0[...].astype(F32)
                m2 = jnp.sum(a * u, axis=-1, keepdims=True) * (1.0 / C)
                m1 = jnp.sum(jnp.where(lane >= 126, u, 0.0), axis=-1, keepdims=True) * (1.0 / C)
                rstd = rs_refs[0][q]
                rhs = jnp.where(lane == 127, m1, a * (rstd * rstd * m2))
                hi = rhs.astype(BF)
                gq[:, C : C + 128] = hi
                gq[:, C + 128 : C + 256] = (rhs - hi.astype(F32)).astype(BF)
                both = dot_at(a0[...], gq[...])
                bb[q * 128 : (q + 1) * 128, :] = both[:, 0:C]
                mm[q] = both[:, C : C + 128] + both[:, C + 128 : C + 256]
                return dsh

            dsh = zero8
            for p in range(4):
                here = dz[:, (p + 1) * C : (p + 2) * C]
                before = dz[:, p * C : (p + 1) * C]
                dsh = one(2 * p, dot_bt(here, weight(1, 0)) + dot_bt(before, weight(1, 2)), dsh)
                dsh = one(2 * p + 1, dot_bt(here, weight(1, 1)), dsh)
                between("first", 0, p)
            dw = jnp.zeros((10, C), F32)
            db = jnp.zeros((1, C), F32)
            dga = jnp.zeros((1, C), F32)
            for q in range(8):
                bq = bb[q * 128 : (q + 1) * 128, :]
                band = wb[:, q * C : (q + 1) * C]
                dga = dga + jnp.sum(bq * band.astype(F32), axis=0, keepdims=True)
                m = mm[q]
                m_hi, m_lo = split(m)
                bandf[...] = bq * g0 - m[:, 127:128] - dot(m_hi.astype(BF), band) - dot(m_lo.astype(BF), band)
                dw = dw + bandf[5 * q : 5 * q + 10, :]
                db = db + bandf[90:91, :]
            small[0:10, :] = dw
            small[10:11, :] = db
            small[17:18, :] = dga * HALF_ROOT
            small[24:25, :] = jnp.sum(dsh, axis=0, keepdims=True) * HALF_ROOT
            small[31:32, :] = jnp.zeros((1, C), F32)


def body_scratch():
    s = [
        pltpu.VMEM((400, 128), BF),
        pltpu.VMEM((4, 3 * C, C), BF),
        pltpu.VMEM((2, 2 * C, C), BF),
        pltpu.VMEM((128, 8 * C), BF),
        pltpu.VMEM((128, 8 * C), BF),
    ]
    s.append([pltpu.VMEM((rows_of[l], in_blocks[l] * C), BF) for l in range(1, 7)])
    s.append([pltpu.VMEM((rows_of[l], phases[l] * C), BF) for l in range(7)])
    s.append([pltpu.VMEM((rows_of[l], phases[l] * C), BF) for l in range(1, 7)])
    s.append([pltpu.VMEM((phases[l], rows_of[l], 128), F32) for l in range(7)])
    s += [
        pltpu.VMEM((400, C), F32),
        pltpu.VMEM((4, 400, C), F32),
        pltpu.VMEM((424, C), F32),
        pltpu.VMEM((4, 424, 128), F32),
        pltpu.VMEM((400, 5 * C), BF),
        pltpu.VMEM((2, 400, C + 256), BF),
        pltpu.VMEM((3 * C, C), F32),
        pltpu.VMEM((8, 128, 128), F32),
        pltpu.VMEM((128, C), F32),
        pltpu.SemaphoreType.DMA((6,)),
    ]
    return s


MESH = pl.DeviceIdType.MESH
SHARD = 32892
ORDERS = (("x", "y", "z"), ("y", "z", "x"), ("z", "x", "y"))


def unit_of(l, k):
    return (l - 1) * 3 + k if l < 5 else 12 + (l - 5) * 2 + k


def order_of(l, k):
    return ORDERS[(k + (2 if l == 6 else 0)) % 3]


def first_tile(d):
    return lax.div(SHARD * d + 3072, 8192) - 1


def encoder_kernel(
    packed, cnt, bal, cot, w1, w3_hbm, w2_hbm, bias, gain, shift, out, *scratch
):
    (a0, w3, w2, wb, gw, xs, dgs, xhs, rss, zs, zt, fs, f4, dz, gn, acc, mm, bandf, wsem,
     small, pk, sb, rb, xr, s0, keep, r0, r1, h2, r2, h3, r3, tl, own, fl, rs0, hs, rs1, ts, far_last, far_zero, hn, near_last, near_zero, sm4,
     sb_sem, rb_sem, s0_sem, r0_sem, s1_sem, r1_sem, s2_sem, r2_sem, s3_sem, r3_sem, t_sem, own_sem,
     q_send, q_recv, root_sem, qr_send) = scratch

    dp = lax.axis_index("dp")
    nw = lax.axis_index("narrow")
    z, y = lax.div(dp, 4), lax.rem(dp, 4)
    x, core = lax.div(nw, 2), lax.rem(nw, 2)
    me = dp * 8 + nw
    at = {"x": x, "y": y, "z": z}

    def peer(axis, delta):
        if axis == "core":
            return (dp, x * 2 + (1 - core))
        if axis == "x":
            return (dp, lax.rem(x + delta, 4) * 2 + core)
        if axis == "y":
            return (z * 4 + lax.rem(y + delta, 4), nw)
        return (lax.rem(z + delta, 4) * 4 + y, nw)

    def remote(src, dst, send, recv, device):
        return pltpu.make_async_remote_copy(
            src_ref=src, dst_ref=dst, send_sem=send, recv_sem=recv, device_id=device, device_id_type=MESH
        )

    barrier = pltpu.get_barrier_semaphore()
    for d in range(1, 8):
        pl.semaphore_signal(barrier, inc=1, device_id=(dp, lax.rem(nw + d, 8)), device_id_type=MESH)
    for axis in ("y", "z"):
        for d in range(1, 4):
            pl.semaphore_signal(barrier, inc=1, device_id=peer(axis, d), device_id_type=MESH)

    def normalise(s):
        n = cnt[s]
        row = lax.broadcasted_iota(jnp.int32, (144, 128), 0)
        lane = lax.broadcasted_iota(jnp.int32, (144, 128), 1)
        block = jnp.where(lane >= 40, 1, 0) + jnp.where(lane >= 80, 1, 0)
        row = row + block * 144
        place = row * 40 + lane - block * 40
        valid = (row < 400) & (lane < 120) & (place < n)
        w = jnp.where(valid, packed[s], 0.0)
        over = jnp.full((1, 1), jnp.maximum(n, 1), jnp.int32).astype(F32)
        total = jnp.sum(jnp.sum(w, axis=0, keepdims=True), axis=1, keepdims=True)
        centred = jnp.where(valid, w - total / over, 0.0)
        square = jnp.sum(jnp.sum(centred * centred, axis=0, keepdims=True), axis=1, keepdims=True)
        value = centred * lax.rsqrt(square / over + 1e-07)
        frames = n
        for k, st in ((10, 5), (3, 2), (3, 2), (3, 2), (3, 2), (2, 2), (2, 2)):
            frames = jnp.maximum(lax.div(frames - k + st, st), 0)
        return jnp.where(lane >= 120, jnp.full((144, 128), frames, jnp.int32).astype(F32), value).astype(BF)

    for s in range(2):
        pk[s] = normalise(s)

    def send_waves():
        for d in range(8):
            there = lax.rem(nw + d, 8)
            m0 = jnp.where(bal[0] == there, 1.0, 0.0)
            m1 = jnp.where(bal[1] == there, 1.0, 0.0)
            sb[d] = (pk[0].astype(F32) * m0 + pk[1].astype(F32) * m1).astype(BF)
        pl.semaphore_wait(barrier, 13)
        copies = []
        for d in range(1, 8):
            c = remote(sb.at[d], rb.at[d - 1], sb_sem.at[d - 1], rb_sem.at[d - 1], (dp, lax.rem(nw + d, 8)))
            c.start()
            copies.append(c)
        return copies

    def route():
        g = sb[0].astype(F32)
        for d in range(1, 8):
            copies[d - 1].wait()
            g = g + rb[d - 1].astype(F32)
        for b in range(3):
            xr[144 * b : 144 * b + 144, :] = g if b == 0 else pltpu.roll(g, 128 - 40 * b, 1)
        xr[432:440, :] = jnp.zeros((8, 128), F32)
        v0 = xr[0:400, :]
        v1 = pltpu.roll(xr[pl.ds(1, 400), :], 40, 1)
        lane = lax.broadcasted_iota(jnp.int32, (400, 128), 1)
        one = jnp.where(lane < 40, v0, jnp.where(lane < 45, v1, 0.0))
        ones = jnp.where((lane >= 90) & (lane < 93), 1.0, 0.0)
        a0[...] = (one + pltpu.roll(one, 45, 1) + ones).astype(BF)
        return g[0:1, 127:128]

    def units(l):
        return [(k, unit_of(l, k), order_of(l, k)) for k in range(taps[l])]

    def slot(l, k):
        return (l % 2) * 3 + k

    def copy0(l, k, u):
        return remote(s0.at[slot(l, k)], r0.at[u], s0_sem.at[u], r0_sem.at[u], peer("core", 1))

    def move0(l, k, acc):
        u, o = unit_of(l, k), order_of(l, k)
        if l + 2 <= 6 and k < taps[l + 2]:
            copy0(l + 2, k, unit_of(l + 2, k)).wait_send()

        def spread(ref, i, half):
            for xx in range(4):
                for yy in range(4):
                    rows = pl.ds(pl.multiple_of(half * 64 + (k * C + xx * 128 + yy * 16), 16), 16)
                    v = acc[rows, :].astype(BF)
                    for zz in range(4):
                        by = {"x": xx, "y": yy, "z": zz}
                        ref[i, by[o[0]], by[o[1]], by[o[2]]] = v[:, zz * 128 : (zz + 1) * 128]

        spread(s0, slot(l, k), 1 - core)
        copy0(l, k, u).start()
        spread(keep, u, core)

    def whole(ref, send, recv, o):
        return remote(ref, ref, send, recv, peer(o, 1))

    def hand_on(buf, got, u, axis, send, recv):
        for d in range(1, 4):
            j = lax.rem(at[axis] + d, 4)
            remote(buf.at[u, j], got.at[u, d - 1], send.at[u], recv.at[u], peer(axis, d)).start()

    def summed(buf, got, u, axis):
        v = buf[u, at[axis]].astype(F32)
        for d in range(3):
            v = v + got[u, d].astype(F32)
        return v.astype(BF)

    def chosen(l, only):
        return [t for t in units(l) if t[0] in only]

    def move1(l, only):
        for k, u, o in chosen(l, only):
            copy0(l, k, u).wait_recv()
            for j in range(4):
                keep[u, j] = (keep[u, j].astype(F32) + r0[u, j].astype(F32)).astype(BF)
            hand_on(keep, r1, u, o[0], s1_sem, r1_sem)

    def move2(l, only):
        for k, u, o in chosen(l, only):
            whole(r1.at[u], s1_sem.at[u], r1_sem.at[u], o[0]).wait_recv()
            h2[u] = summed(keep, r1, u, o[0])
            hand_on(h2, r2, u, o[1], s2_sem, r2_sem)

    def move3(l, only):
        for k, u, o in chosen(l, only):
            whole(r2.at[u], s2_sem.at[u], r2_sem.at[u], o[1]).wait_recv()
            h3[u] = summed(h2, r2, u, o[1])
            hand_on(h3, r3, u, o[2], s3_sem, r3_sem)

    def owners(u):
        tile = u * 32 + x * 8 + core * 4 + y
        start = (10 + 16 * tile) * C
        first = lax.div(start, SHARD)
        last = lax.div(start + 8191, SHARD)
        return tile, ((first, True), (last, last != first))

    def final(u, i, tile, d):
        s = tile - first_tile(d)
        device = (lax.div(d, 8), lax.rem(d, 8))
        return remote(tl.at[u], own.at[s, z], t_sem.at[u, i], own_sem.at[s], device)

    def final_here(u, tile, d):
        return pltpu.make_async_copy(tl.at[u], own.at[tile - first_tile(d), z], own_sem.at[tile - first_tile(d)])

    def move4(l, only):
        for k, u, o in chosen(l, only):
            whole(r3.at[u], s3_sem.at[u], r3_sem.at[u], o[2]).wait_recv()
            tl[u] = summed(h3, r3, u, o[2])
            tile, targets = owners(u)
            for i, (d, wanted) in enumerate(targets):
                @pl.when(jnp.logical_and(wanted, d != me))
                def _(u=u, i=i, tile=tile, d=d):
                    final(u, i, tile, d).start()

                @pl.when(jnp.logical_and(wanted, d == me))
                def _(u=u, tile=tile, d=d):
                    final_here(u, tile, d).start()

    def emit(l, k, acc):
        move0(l, k, acc)

    plan = {
        ("wgrad", 4, 0): [(move1, 6)],
        ("wgrad", 3, 0): [(move1, 5)],
        ("back", 2, 1): [(move1, 4)],
        ("back", 1, 0): [(move1, 3)],
        ("back", 1, 3): [(move1, 2), (move2, 6), (move2, 5)],
        ("wgrad", 1, 0): [(move2, 4)],
        ("first", 0, 0): [(move1, 1), (move3, 6), (move3, 5), (move2, 3)],
        ("first", 0, 1): [(move3, 4)],
        ("first", 0, 2): [(move2, 2), (move3, 3), (move4, 6), (move4, 5)],
        ("first", 0, 3): [(move4, 4)],
    }

    def between(kind, l, p):
        for move, layer, *only in plan.get((kind, l, p), ()):
            move(layer, only[0] if only else (0, 1, 2))

    fl[...] = jnp.zeros_like(fl)
    copies = send_waves()
    encoder_body(
        route, cot, w1, w3_hbm, w2_hbm, bias, gain, shift, emit, between, small,
        a0, w3, w2, wb, gw, [None] + list(xs), list(dgs), [None] + list(xhs), list(rss),
        zs, zt, fs, f4, dz, gn, acc, acc, mm, bandf, wsem,
    )

    def rows_of_core(c):
        return pl.ds(pl.multiple_of(c * 16, 16), 16)

    c0 = remote(small.at[rows_of_core(1 - core)], rs0, q_send.at[0], q_recv.at[0], peer("core", 1))
    c0.start()
    move2(1, (0, 1, 2))
    move3(2, (0, 1, 2))
    c0.wait()
    v = small[rows_of_core(core), :] + rs0[...]
    for c in range(4):
        hs[c] = v[:, c * 128 : (c + 1) * 128]
    cx = []
    for d in range(1, 4):
        c1 = remote(hs.at[lax.rem(x + d, 4)], rs1.at[d - 1], q_send.at[d], q_recv.at[d], peer("x", d))
        c1.start()
        cx.append(c1)
    move3(1, (0, 1, 2))
    move4(3, (0, 1, 2))
    move4(2, (0, 1, 2))
    v = hs[x]
    for d in range(3):
        cx[d].wait()
        v = v + rs1[d]
    ts[...] = v
    at_last, at_zero = dp == 15, jnp.logical_and(dp == 0, core == 0)
    is_last, is_zero = me == 127, me == 0
    to_last = remote(ts, far_last.at[dp], qr_send.at[0], root_sem.at[0], (15, nw))
    to_zero = remote(ts, far_zero.at[dp], qr_send.at[1], root_sem.at[1], (0, nw))
    sends_zero = jnp.logical_and(core == 0, dp != 0)

    @pl.when(dp != 15)
    def _():
        to_last.start()

    @pl.when(sends_zero)
    def _():
        to_zero.start()

    move4(1, (0, 1, 2))
    in_last = remote(hn.at[0], near_last.at[nw], qr_send.at[2], root_sem.at[2], (15, 7))
    in_zero = remote(hn.at[1], near_zero.at[x], qr_send.at[3], root_sem.at[3], (0, 0))

    @pl.when(at_last)
    def _():
        pltpu.make_async_copy(far_last.at[0:15], far_last.at[0:15], root_sem.at[0]).wait()
        v = ts[...]
        for i in range(15):
            v = v + far_last[i]
        hn[0] = v

        @pl.when(nw != 7)
        def _():
            in_last.start()

        @pl.when(nw == 7)
        def _():
            near_last[7] = v

    @pl.when(at_zero)
    def _():
        pltpu.make_async_copy(far_zero.at[1:16], far_zero.at[1:16], root_sem.at[1]).wait()
        v = ts[...]
        for i in range(1, 16):
            v = v + far_zero[i]
        hn[1] = v

        @pl.when(x != 0)
        def _():
            in_zero.start()

        @pl.when(x == 0)
        def _():
            near_zero[0] = v

    low = first_tile(me)
    high = jnp.minimum(lax.div(SHARD * me + SHARD - 1 + 3072, 8192) - 1, 511)

    for s in range(6):
        @pl.when(jnp.logical_and(low + s >= 0, low + s <= high))
        def _(s=s):
            pltpu.make_async_copy(own.at[s], own.at[s], own_sem.at[s]).wait()
            for c in range(4):
                fl[pl.ds(64 * s + c, 16, stride=4), :] = own[s, c].astype(F32)

    @pl.when(is_last)
    def _():
        pltpu.make_async_copy(near_last.at[0:7], near_last.at[0:7], root_sem.at[2]).wait()
        for c in range(4):
            for h in range(2):
                sm4[c, 16 * h : 16 * h + 16, :] = near_last[2 * c + h]
            fl[pl.ds(192 + c, 21, stride=4), :] = sm4[c, 10:31, :]

    @pl.when(is_zero)
    def _():
        pltpu.make_async_copy(near_zero.at[1:4], near_zero.at[1:4], root_sem.at[3]).wait()
        for c in range(4):
            sm4[c, 0:16, :] = near_zero[c]
            fl[pl.ds(24 + c, 10, stride=4), :] = sm4[c, 0:10, :]

    offset = SHARD * me - C * (10 + 16 * low)
    row = lax.div(offset, 128)
    turn = lax.rem(offset, 128)
    back = lax.rem(128 - turn, 128)
    upper = pltpu.roll(fl[pl.ds(row, 264), :], back, 1)
    lower = pltpu.roll(fl[pl.ds(row + 1, 264), :], back, 1)
    lane = lax.broadcasted_iota(jnp.int32, (264, 128), 1)
    out[...] = jnp.where(lane < 128 - turn, upper, lower)

    for l in range(1, 7):
        for k, u, o in units(l):
            if l <= 2:
                copy0(l, k, u).wait_send()
            elif k >= taps[l - 2]:
                copy0(l, k, u).wait_send()
            whole(r1.at[u], s1_sem.at[u], r1_sem.at[u], o[0]).wait_send()
            whole(r2.at[u], s2_sem.at[u], r2_sem.at[u], o[1]).wait_send()
            whole(r3.at[u], s3_sem.at[u], r3_sem.at[u], o[2]).wait_send()
            tile, targets = owners(u)
            for i, (d, wanted) in enumerate(targets):
                @pl.when(jnp.logical_and(wanted, d != me))
                def _(u=u, i=i, tile=tile, d=d):
                    final(u, i, tile, d).wait_send()

    @pl.when(dp != 15)
    def _():
        to_last.wait_send()

    @pl.when(sends_zero)
    def _():
        to_zero.wait_send()

    @pl.when(jnp.logical_and(at_last, nw != 7))
    def _():
        in_last.wait_send()

    @pl.when(jnp.logical_and(at_zero, x != 0))
    def _():
        in_zero.wait_send()


def comm_scratch():
    dma = pltpu.SemaphoreType.DMA
    return [
        pltpu.VMEM((32, C), F32),
        pltpu.VMEM((2, 144, 128), BF),
        pltpu.VMEM((8, 144, 128), BF),
        pltpu.VMEM((7, 144, 128), BF),
        pltpu.VMEM((440, 128), F32),
        pltpu.VMEM((6, 4, 4, 4, 16, 128), BF),
        pltpu.VMEM((16, 4, 4, 4, 16, 128), BF),
        pltpu.VMEM((16, 4, 4, 4, 16, 128), BF),
        pltpu.VMEM((16, 3, 4, 4, 16, 128), BF),
        pltpu.VMEM((16, 4, 4, 16, 128), BF),
        pltpu.VMEM((16, 3, 4, 16, 128), BF),
        pltpu.VMEM((16, 4, 16, 128), BF),
        pltpu.VMEM((16, 3, 16, 128), BF),
        pltpu.VMEM((16, 16, 128), BF),
        pltpu.VMEM((6, 4, 16, 128), BF),
        pltpu.VMEM((392, 128), F32),
        pltpu.VMEM((16, C), F32),
        pltpu.VMEM((4, 16, 128), F32),
        pltpu.VMEM((3, 16, 128), F32),
        pltpu.VMEM((16, 128), F32),
        pltpu.VMEM((16, 16, 128), F32),
        pltpu.VMEM((16, 16, 128), F32),
        pltpu.VMEM((2, 16, 128), F32),
        pltpu.VMEM((8, 16, 128), F32),
        pltpu.VMEM((4, 16, 128), F32),
        pltpu.VMEM((4, 32, 128), F32),
        dma((7,)), dma((7,)),
        dma((16,)), dma((16,)), dma((16,)), dma((16,)), dma((16,)), dma((16,)), dma((16,)), dma((16,)),
        dma((16, 2)), dma((6,)),
        dma((4,)), dma((4,)), dma((4,)), dma((4,)),
    ]


def encoder_call(packed, cnt, bal, cot, w1, w3, w2, bias, gain, shift):
    vm = pl.BlockSpec(memory_space=pltpu.VMEM)
    sm = pl.BlockSpec(memory_space=pltpu.SMEM)
    hb = pl.BlockSpec(memory_space=pl.ANY)
    return pl.pallas_call(
        encoder_kernel,
        out_shape=jax.ShapeDtypeStruct((264, 128), F32),
        in_specs=[vm, sm, sm, vm, vm, hb, hb, vm, vm, vm],
        out_specs=vm,
        scratch_shapes=body_scratch() + comm_scratch(),
        compiler_params=pltpu.CompilerParams(
            vmem_limit_bytes=64 * 1024 * 1024 - 1024 * 64, collective_id=0, has_side_effects=True
        ),
    )(packed, cnt, bal, cot, w1, w3, w2, bias, gain, shift)


def pack_waves(waves):
    r = jnp.pad(waves.reshape(2, 400, 40), ((0, 0), (0, 32), (0, 0)))
    r = r.reshape(2, 3, 144, 40).transpose(0, 2, 1, 3).reshape(2, 144, 120)
    return jnp.pad(r, ((0, 0), (0, 0), (0, 8)))


def on_device(waveforms, valid_counts, balance_list, cotangent, w_first, w_three, w_two, conv_bias, norm_gain, norm_shift):
    shard = encoder_call(
        pack_waves(waveforms), valid_counts, balance_list, cotangent, w_first,
        w_three.reshape(4, 3 * C, C), w_two.reshape(2, 2 * C, C), conv_bias, norm_gain, norm_shift,
    )
    return shard.reshape(-1)[:SHARD]


def solution(mesh):
    both = ("dp", "narrow")
    in_specs = (
        P(both, None), P(both), P(both), P(both, None, None),
        P(), P(), P(), P(), P(), P(),
    )
    return jax.shard_map(on_device, mesh=mesh, in_specs=in_specs, out_specs=P(both), check_vma=False)
```

```python
import jax
import jax.numpy as jnp
from jax import lax
from jax.experimental import pallas as pl
from jax.experimental.pallas import tpu as pltpu
from jax.sharding import PartitionSpec as P

C = 512
F7 = 49
BF = jnp.bfloat16
F32 = jnp.float32

taps = (None, 3, 3, 3, 3, 2, 2)
phases = (8, 4, 2, 1, 1, 1, 1)
rows_of = (400, 400, 400, 400, 208, 112, 64)
in_blocks = (None, 9, 5, 3, 3, 2, 2)
ROW_TILE = {400: 400, 208: 208, 112: 112, 64: 64}


def dot(a, b):
    return jnp.dot(a, b, preferred_element_type=F32)


def dot_bt(a, b):
    return lax.dot_general(a, b, (((1,), (1,)), ((), ())), preferred_element_type=F32)


def dot_at(a, b):
    return lax.dot_general(a, b, (((0,), (0,)), ((), ())), preferred_element_type=F32)


HALF_ROOT = 0.7071067811865476
LOG2E = 1.4426950408889634
LOG2_C = -0.3257480647361593


def gelu_pair(m):
    phi = HALF_ROOT + HALF_ROOT * lax.erf(m)
    e = jnp.exp2(LOG2_C - (m * m) * LOG2E)
    return m * phi, phi + m * e


def loop_rows(rows, body, init):
    tile = ROW_TILE[rows]

    def step(i, carry):
        return body(pl.ds(pl.multiple_of(i * tile, tile), tile), carry)

    return lax.fori_loop(0, rows // tile, step, init)


def fold8(v):
    total = v[0:8]
    for i in range(8, v.shape[0], 8):
        total = total + v[i : i + 8]
    return total


def encoder_body(
    route, cot, w1, w3_hbm, w2_hbm, bias, gain, shift,
    emit, between, small,
    a0, w3, w2, wb, gw, x_refs, dg_refs, xh_refs, rs_refs, zs, zt, fs, f4, dz, gn, acc, bb, mm, bandf, wsem,
):
    w_copies = []
    for i in range(4):
        w_copies.append(pltpu.make_async_copy(w3_hbm.at[i], w3.at[i], wsem.at[i]))
    for i in range(2):
        w_copies.append(pltpu.make_async_copy(w2_hbm.at[i], w2.at[i], wsem.at[4 + i]))
    for c in w_copies:
        c.start()

    def weight(l, k):
        if l < 5:
            return w3[l - 1, k * C : (k + 1) * C, :]
        return w2[l - 5, k * C : (k + 1) * C, :]

    wf = w1[...].astype(F32)
    wc = wf - jnp.mean(wf, axis=-1, keepdims=True)
    b0 = bias[0:1, :]
    bc = b0 - jnp.mean(b0, axis=-1, keepdims=True)
    g0 = gain[0:1, :] * HALF_ROOT

    def split(v):
        hi = v.astype(BF).astype(F32)
        return hi, v - hi

    wc_hi, wc_lo = split(wc)
    bc_hi, bc_r = split(bc)
    bc_mid, bc_lo = split(bc_r)
    gw_hi, gw_lo = split(wc * g0)
    gb_hi, gb_lo = split(bc * g0)
    g_hi, g_lo = split(g0)
    for p in range(8):
        bandf[...] = jnp.zeros_like(bandf)
        bandf[5 * p : 5 * p + 10, :] = wc_hi
        bandf[45 + 5 * p : 55 + 5 * p, :] = wc_lo
        bandf[90:91, :] = bc_hi
        bandf[91:92, :] = bc_mid
        bandf[92:93, :] = bc_lo
        wb[:, p * C : (p + 1) * C] = bandf[...].astype(BF)
        bandf[5 * p : 5 * p + 10, :] = gw_hi
        bandf[45 + 5 * p : 55 + 5 * p, :] = gw_lo
        bandf[90:91, :] = gb_hi
        bandf[91:92, :] = gb_lo
        bandf[92:93, :] = jnp.zeros_like(bc_lo)
        bandf[126:127, :] = g_hi
        bandf[127:128, :] = g_lo
        gw[:, p * C : (p + 1) * C] = bandf[...].astype(BF)

    fs[400:424, :] = jnp.zeros((24, C), F32)
    f4[:, 400:424, :] = jnp.zeros((4, 24, 128), F32)

    last_frames = route()

    def activate(l, p, centred, zs):
        rows = rows_of[l]
        lanes = slice(p * C, (p + 1) * C)
        b = bias[l : l + 1, :]
        g = gain[l : l + 1, :] * HALF_ROOT
        s = shift[l : l + 1, :] * HALF_ROOT

        def body(r, carry):
            z = zs[r, :]
            if not centred:
                z = z + b
                z = z - jnp.sum(z, axis=-1, keepdims=True) * (1.0 / C)
            var = jnp.sum(z * z, axis=-1, keepdims=True) * (1.0 / C)
            rstd = lax.rsqrt(var + 1e-05)
            xh = z * rstd
            x, d = gelu_pair(xh * g + s)
            dg_refs[l][r, lanes] = d.astype(BF)
            if l > 0:
                xh_refs[l][r, lanes] = xh.astype(BF)
            rs_refs[l][p, r, :] = jnp.broadcast_to(rstd, (rstd.shape[0], 128))
            if l < 3:
                x_refs[l + 1][r, lanes] = x.astype(BF)
            if l < 3 and p == 0:
                fs[r, :] = x
            elif l < 6:
                for c in range(4):
                    f4[c, r, :] = x[:, c * 128 : (c + 1) * 128]
            return carry

        loop_rows(rows, body, 0)
        if l < 3 and p == 0:
            n = phases[l]
            x_refs[l + 1][:, n * C : (n + 1) * C] = fs[pl.ds(1, 400), :].astype(BF)

    for p in range(8):
        zt[p % 4] = dot(a0[...], wb[:, p * C : (p + 1) * C])
        activate(0, p, True, zt.at[p % 4])

    for l in range(1, 7):
        w_copies[l - 1].wait()
        k, rows = taps[l], rows_of[l]
        for p in range(phases[l]):
            w = w3[l - 1] if l < 5 else w2[l - 5]
            zt[p, 0:rows, :] = dot(x_refs[l][:, p * 2 * C : (p * 2 + k) * C], w)
            activate(l, p, False, zt.at[p])
        if 3 <= l < 6:
            n = rows_of[l + 1]
            for j in range(taps[l + 1]):
                for c in range(4):
                    x_refs[l + 1][:, j * C + c * 128 : j * C + (c + 1) * 128] = f4[
                        c, pl.ds(j, n, stride=2), :
                    ].astype(BF)

    row_id = lax.broadcasted_iota(jnp.int32, (F7, C), 0).astype(F32)
    zs[0:64, :] = jnp.zeros((64, C), F32)
    zs[0:F7, :] = jnp.where(row_id < last_frames, cot[0].astype(F32), 0.0)

    def got(src, r):
        if src is None:
            return jnp.concatenate([f4[c, r, :] for c in range(4)], axis=-1)
        return src[r, :]

    def norm_back(l, p, src, sums):
        lanes = slice(p * C, (p + 1) * C)
        out = slice((p + 1) * C, (p + 2) * C)
        g = gain[l : l + 1, :] * HALF_ROOT

        def body(r, carry):
            db, dga, dsh = carry
            gv = got(src, r) * dg_refs[l][r, lanes].astype(F32)
            xh = xh_refs[l][r, lanes].astype(F32)
            rstd = rs_refs[l][p, r, :][:, 0:1]
            dsh = dsh + fold8(gv)
            dga = dga + fold8(gv * xh)
            gx = gv * g
            m1 = jnp.sum(gx, axis=-1, keepdims=True) * (1.0 / C)
            m2 = jnp.sum(gx * xh, axis=-1, keepdims=True) * (1.0 / C)
            d = (gx - m1 - xh * m2) * rstd
            db = db + fold8(d)
            dz[r, out] = d.astype(BF)
            return db, dga, dsh

        return loop_rows(rows_of[l], body, sums)

    zero8 = jnp.zeros((8, C), F32)
    sums = norm_back(6, 0, zs, (zero8, zero8, zero8))

    def store_sums(l, sums):
        for j in range(3):
            total = jnp.sum(sums[j], axis=0, keepdims=True)
            small[10 + 7 * j + l : 11 + 7 * j + l, :] = total if j == 0 else total * HALF_ROOT

    for l in range(6, 0, -1):
        k, rows, n = taps[l], rows_of[l], phases[l]
        store_sums(l, sums)
        if k == 3:
            fs[8 : 8 + rows, :] = dz[0:rows, n * C : (n + 1) * C].astype(F32)
            fs[0:8, :] = jnp.zeros((8, C), F32)
            dz[0:rows, 0:C] = fs[pl.ds(7, rows), :].astype(BF)

        for j in range(k):
            for p in range(n):
                part = dot_at(
                    x_refs[l][:, (2 * p + j) * C : (2 * p + j + 1) * C], dz[0:rows, (p + 1) * C : (p + 2) * C]
                )
                if p == 0:
                    acc[j * C : (j + 1) * C, :] = part
                else:
                    acc[j * C : (j + 1) * C, :] += part
            emit(l, j, acc)
        between("wgrad", l, 0)

        if l > 3:
            here = dz[0:rows, C : 2 * C]
            even = dot_bt(here, weight(l, 0))
            if k == 3:
                even = even + dot_bt(dz[0:rows, 0:C], weight(l, 2))
            odd = dot_bt(here, weight(l, 1))
            half = rows_of[l - 1] // 2
            for c in range(4):
                f4[c, pl.ds(0, half, stride=2), :] = even[:half, c * 128 : (c + 1) * 128]
                f4[c, pl.ds(1, half, stride=2), :] = odd[:half, c * 128 : (c + 1) * 128]
            sums = norm_back(l - 1, 0, None, (zero8, zero8, zero8))
            between("back", l - 1, 0)
        elif l > 1:
            def dgrad(p, carry, l=l):
                here = dz[:, pl.ds(pl.multiple_of((p + 1) * C, C), C)]
                before = dz[:, pl.ds(pl.multiple_of(p * C, C), C)]
                zt[2 * p] = dot_bt(here, weight(l, 0)) + dot_bt(before, weight(l, 2))
                zt[2 * p + 1] = dot_bt(here, weight(l, 1))
                return carry

            for p in range(n):
                dgrad(p, 0)

            def back(p, carry, l=l):
                return norm_back(l - 1, p, zt.at[p], carry)

            sums = (zero8, zero8, zero8)
            for p in range(2 * n):
                sums = back(p, sums)
                between("back", l - 1, p)
        else:
            lane = lax.broadcasted_iota(jnp.int32, (400, 128), 1)

            def one(q, src, dsh):
                lanes = slice(q * C, (q + 1) * C)
                zq, gq = zt.at[q % 4], gn.at[q % 2]
                zq[...] = src

                def body(r, dsh):
                    gv = zq[r, :] * dg_refs[0][r, lanes].astype(F32)
                    gq[r, 0:C] = (gv * rs_refs[0][q, r, :][:, 0:1]).astype(BF)
                    return dsh + fold8(gv)

                dsh = loop_rows(400, body, dsh)
                u = dot_bt(gq[:, 0:C], gw[:, lanes])
                a = a0[...].astype(F32)
                m2 = jnp.sum(a * u, axis=-1, keepdims=True) * (1.0 / C)
                m1 = jnp.sum(jnp.where(lane >= 126, u, 0.0), axis=-1, keepdims=True) * (1.0 / C)
                rstd = rs_refs[0][q]
                rhs = jnp.where(lane == 127, m1, a * (rstd * rstd * m2))
                hi = rhs.astype(BF)
                gq[:, C : C + 128] = hi
                gq[:, C + 128 : C + 256] = (rhs - hi.astype(F32)).astype(BF)
                both = dot_at(a0[...], gq[...])
                bb[q * 128 : (q + 1) * 128, :] = both[:, 0:C]
                mm[q] = both[:, C : C + 128] + both[:, C + 128 : C + 256]
                return dsh

            dsh = zero8
            for p in range(4):
                here = dz[:, (p + 1) * C : (p + 2) * C]
                before = dz[:, p * C : (p + 1) * C]
                dsh = one(2 * p, dot_bt(here, weight(1, 0)) + dot_bt(before, weight(1, 2)), dsh)
                dsh = one(2 * p + 1, dot_bt(here, weight(1, 1)), dsh)
                between("first", 0, p)
            dw = jnp.zeros((10, C), F32)
            db = jnp.zeros((1, C), F32)
            dga = jnp.zeros((1, C), F32)
            for q in range(8):
                bq = bb[q * 128 : (q + 1) * 128, :]
                band = wb[:, q * C : (q + 1) * C]
                dga = dga + jnp.sum(bq * band.astype(F32), axis=0, keepdims=True)
                m = mm[q]
                m_hi, m_lo = split(m)
                bandf[...] = bq * g0 - m[:, 127:128] - dot(m_hi.astype(BF), band) - dot(m_lo.astype(BF), band)
                dw = dw + bandf[5 * q : 5 * q + 10, :]
                db = db + bandf[90:91, :]
            small[0:10, :] = dw
            small[10:11, :] = db
            small[17:18, :] = dga * HALF_ROOT
            small[24:25, :] = jnp.sum(dsh, axis=0, keepdims=True) * HALF_ROOT
            small[31:32, :] = jnp.zeros((1, C), F32)


def body_scratch():
    s = [
        pltpu.VMEM((400, 128), BF),
        pltpu.VMEM((4, 3 * C, C), BF),
        pltpu.VMEM((2, 2 * C, C), BF),
        pltpu.VMEM((128, 8 * C), BF),
        pltpu.VMEM((128, 8 * C), BF),
    ]
    s.append([pltpu.VMEM((rows_of[l], in_blocks[l] * C), BF) for l in range(1, 7)])
    s.append([pltpu.VMEM((rows_of[l], phases[l] * C), BF) for l in range(7)])
    s.append([pltpu.VMEM((rows_of[l], phases[l] * C), BF) for l in range(1, 7)])
    s.append([pltpu.VMEM((phases[l], rows_of[l], 128), F32) for l in range(7)])
    s += [
        pltpu.VMEM((400, C), F32),
        pltpu.VMEM((4, 400, C), F32),
        pltpu.VMEM((424, C), F32),
        pltpu.VMEM((4, 424, 128), F32),
        pltpu.VMEM((400, 5 * C), BF),
        pltpu.VMEM((2, 400, C + 256), BF),
        pltpu.VMEM((3 * C, C), F32),
        pltpu.VMEM((8, 128, 128), F32),
        pltpu.VMEM((128, C), F32),
        pltpu.SemaphoreType.DMA((6,)),
    ]
    return s


MESH = pl.DeviceIdType.MESH
SHARD = 32892
ORDERS = (("x", "y", "z"), ("y", "z", "x"), ("z", "x", "y"))


def unit_of(l, k):
    return (l - 1) * 3 + k if l < 5 else 12 + (l - 5) * 2 + k


def order_of(l, k):
    return ORDERS[(k + (2 if l == 6 else 0)) % 3]


def first_tile(d):
    return lax.div(SHARD * d + 3072, 8192) - 1


def encoder_kernel(
    packed, cnt, bal, cot, w1, w3_hbm, w2_hbm, bias, gain, shift, out, *scratch
):
    (a0, w3, w2, wb, gw, xs, dgs, xhs, rss, zs, zt, fs, f4, dz, gn, acc, mm, bandf, wsem,
     small, pk, sb, rb, xr, s0, keep, r0, r1, h2, r2, h3, r3, tl, own, fl, rs0, hs, rs1, ts, far_last, far_zero, hn, near_last, near_zero, sm4,
     sb_sem, rb_sem, s0_sem, r0_sem, s1_sem, r1_sem, s2_sem, r2_sem, s3_sem, r3_sem, t_sem, own_sem,
     q_send, q_recv, root_sem, qr_send) = scratch

    dp = lax.axis_index("dp")
    nw = lax.axis_index("narrow")
    z, y = lax.div(dp, 4), lax.rem(dp, 4)
    x, core = lax.div(nw, 2), lax.rem(nw, 2)
    me = dp * 8 + nw
    at = {"x": x, "y": y, "z": z}

    def peer(axis, delta):
        if axis == "core":
            return (dp, x * 2 + (1 - core))
        if axis == "x":
            return (dp, lax.rem(x + delta, 4) * 2 + core)
        if axis == "y":
            return (z * 4 + lax.rem(y + delta, 4), nw)
        return (lax.rem(z + delta, 4) * 4 + y, nw)

    def remote(src, dst, send, recv, device):
        return pltpu.make_async_remote_copy(
            src_ref=src, dst_ref=dst, send_sem=send, recv_sem=recv, device_id=device, device_id_type=MESH
        )

    barrier = pltpu.get_barrier_semaphore()
    for d in range(1, 8):
        pl.semaphore_signal(barrier, inc=1, device_id=(dp, lax.rem(nw + d, 8)), device_id_type=MESH)
    for axis in ("y", "z"):
        for d in range(1, 4):
            pl.semaphore_signal(barrier, inc=1, device_id=peer(axis, d), device_id_type=MESH)

    def normalise(s):
        n = cnt[s]
        row = lax.broadcasted_iota(jnp.int32, (144, 128), 0)
        lane = lax.broadcasted_iota(jnp.int32, (144, 128), 1)
        block = jnp.where(lane >= 40, 1, 0) + jnp.where(lane >= 80, 1, 0)
        row = row + block * 144
        place = row * 40 + lane - block * 40
        valid = (row < 400) & (lane < 120) & (place < n)
        w = jnp.where(valid, packed[s], 0.0)
        over = jnp.full((1, 1), jnp.maximum(n, 1), jnp.int32).astype(F32)
        total = jnp.sum(jnp.sum(w, axis=0, keepdims=True), axis=1, keepdims=True)
        centred = jnp.where(valid, w - total / over, 0.0)
        square = jnp.sum(jnp.sum(centred * centred, axis=0, keepdims=True), axis=1, keepdims=True)
        value = centred * lax.rsqrt(square / over + 1e-07)
        frames = n
        for k, st in ((10, 5), (3, 2), (3, 2), (3, 2), (3, 2), (2, 2), (2, 2)):
            frames = jnp.maximum(lax.div(frames - k + st, st), 0)
        return jnp.where(lane >= 120, jnp.full((144, 128), frames, jnp.int32).astype(F32), value).astype(BF)

    for s in range(2):
        pk[s] = normalise(s)

    def send_waves():
        for d in range(8):
            there = lax.rem(nw + d, 8)
            m0 = jnp.where(bal[0] == there, 1.0, 0.0)
            m1 = jnp.where(bal[1] == there, 1.0, 0.0)
            sb[d] = (pk[0].astype(F32) * m0 + pk[1].astype(F32) * m1).astype(BF)
        pl.semaphore_wait(barrier, 13)
        copies = []
        for d in range(1, 8):
            c = remote(sb.at[d], rb.at[d - 1], sb_sem.at[d - 1], rb_sem.at[d - 1], (dp, lax.rem(nw + d, 8)))
            c.start()
            copies.append(c)
        return copies

    def route():
        g = sb[0].astype(F32)
        for d in range(1, 8):
            copies[d - 1].wait()
            g = g + rb[d - 1].astype(F32)
        for b in range(3):
            xr[144 * b : 144 * b + 144, :] = g if b == 0 else pltpu.roll(g, 128 - 40 * b, 1)
        xr[432:440, :] = jnp.zeros((8, 128), F32)
        v0 = xr[0:400, :]
        v1 = pltpu.roll(xr[pl.ds(1, 400), :], 40, 1)
        lane = lax.broadcasted_iota(jnp.int32, (400, 128), 1)
        one = jnp.where(lane < 40, v0, jnp.where(lane < 45, v1, 0.0))
        ones = jnp.where((lane >= 90) & (lane < 93), 1.0, 0.0)
        a0[...] = (one + pltpu.roll(one, 45, 1) + ones).astype(BF)
        return g[0:1, 127:128]

    def units(l):
        return [(k, unit_of(l, k), order_of(l, k)) for k in range(taps[l])]

    def slot(l, k):
        return (l % 2) * 3 + k

    def copy0(l, k, u):
        return remote(s0.at[slot(l, k)], r0.at[u], s0_sem.at[u], r0_sem.at[u], peer("core", 1))

    def move0(l, k, acc):
        u, o = unit_of(l, k), order_of(l, k)
        if l + 2 <= 6 and k < taps[l + 2]:
            copy0(l + 2, k, unit_of(l + 2, k)).wait_send()

        def spread(ref, i, half):
            for xx in range(4):
                for yy in range(4):
                    rows = pl.ds(pl.multiple_of(half * 64 + (k * C + xx * 128 + yy * 16), 16), 16)
                    v = acc[rows, :].astype(BF)
                    for zz in range(4):
                        by = {"x": xx, "y": yy, "z": zz}
                        ref[i, by[o[0]], by[o[1]], by[o[2]]] = v[:, zz * 128 : (zz + 1) * 128]

        spread(s0, slot(l, k), 1 - core)
        copy0(l, k, u).start()
        spread(keep, u, core)

    def whole(ref, send, recv, o):
        return remote(ref, ref, send, recv, peer(o, 1))

    def hand_on(buf, got, u, axis, send, recv):
        for d in range(1, 4):
            j = lax.rem(at[axis] + d, 4)
            remote(buf.at[u, j], got.at[u, d - 1], send.at[u], recv.at[u], peer(axis, d)).start()

    def summed(buf, got, u, axis):
        v = buf[u, at[axis]].astype(F32)
        for d in range(3):
            v = v + got[u, d].astype(F32)
        return v.astype(BF)

    def chosen(l, only):
        return [t for t in units(l) if t[0] in only]

    def move1(l, only):
        for k, u, o in chosen(l, only):
            copy0(l, k, u).wait_recv()
            for j in range(4):
                keep[u, j] = (keep[u, j].astype(F32) + r0[u, j].astype(F32)).astype(BF)
            hand_on(keep, r1, u, o[0], s1_sem, r1_sem)

    def move2(l, only):
        for k, u, o in chosen(l, only):
            whole(r1.at[u], s1_sem.at[u], r1_sem.at[u], o[0]).wait_recv()
            h2[u] = summed(keep, r1, u, o[0])
            hand_on(h2, r2, u, o[1], s2_sem, r2_sem)

    def move3(l, only):
        for k, u, o in chosen(l, only):
            whole(r2.at[u], s2_sem.at[u], r2_sem.at[u], o[1]).wait_recv()
            h3[u] = summed(h2, r2, u, o[1])
            hand_on(h3, r3, u, o[2], s3_sem, r3_sem)

    def owners(u):
        tile = u * 32 + x * 8 + core * 4 + y
        start = (10 + 16 * tile) * C
        first = lax.div(start, SHARD)
        last = lax.div(start + 8191, SHARD)
        return tile, ((first, True), (last, last != first))

    def final(u, i, tile, d):
        s = tile - first_tile(d)
        device = (lax.div(d, 8), lax.rem(d, 8))
        return remote(tl.at[u], own.at[s, z], t_sem.at[u, i], own_sem.at[s], device)

    def final_here(u, tile, d):
        return pltpu.make_async_copy(tl.at[u], own.at[tile - first_tile(d), z], own_sem.at[tile - first_tile(d)])

    def move4(l, only):
        for k, u, o in chosen(l, only):
            whole(r3.at[u], s3_sem.at[u], r3_sem.at[u], o[2]).wait_recv()
            tl[u] = summed(h3, r3, u, o[2])
            tile, targets = owners(u)
            for i, (d, wanted) in enumerate(targets):
                @pl.when(jnp.logical_and(wanted, d != me))
                def _(u=u, i=i, tile=tile, d=d):
                    final(u, i, tile, d).start()

                @pl.when(jnp.logical_and(wanted, d == me))
                def _(u=u, tile=tile, d=d):
                    final_here(u, tile, d).start()

    def emit(l, k, acc):
        move0(l, k, acc)

    plan = {
        ("wgrad", 4, 0): [(move1, 6)],
        ("wgrad", 3, 0): [(move1, 5)],
        ("back", 2, 1): [(move1, 4)],
        ("back", 1, 0): [(move1, 3)],
        ("back", 1, 3): [(move1, 2), (move2, 6), (move2, 5)],
        ("wgrad", 1, 0): [(move2, 4)],
        ("first", 0, 0): [(move1, 1), (move3, 6), (move3, 5), (move2, 3)],
        ("first", 0, 1): [(move3, 4)],
        ("first", 0, 2): [(move2, 2), (move3, 3), (move4, 6), (move4, 5)],
        ("first", 0, 3): [(move2, 1), (move4, 4)],
    }

    def between(kind, l, p):
        for move, layer, *only in plan.get((kind, l, p), ()):
            move(layer, only[0] if only else (0, 1, 2))

    fl[...] = jnp.zeros_like(fl)
    copies = send_waves()
    encoder_body(
        route, cot, w1, w3_hbm, w2_hbm, bias, gain, shift, emit, between, small,
        a0, w3, w2, wb, gw, [None] + list(xs), list(dgs), [None] + list(xhs), list(rss),
        zs, zt, fs, f4, dz, gn, acc, acc, mm, bandf, wsem,
    )

    def rows_of_core(c):
        return pl.ds(pl.multiple_of(c * 16, 16), 16)

    c0 = remote(small.at[rows_of_core(1 - core)], rs0, q_send.at[0], q_recv.at[0], peer("core", 1))
    c0.start()
    move3(2, (0, 1, 2))
    c0.wait()
    v = small[rows_of_core(core), :] + rs0[...]
    for c in range(4):
        hs[c] = v[:, c * 128 : (c + 1) * 128]
    cx = []
    for d in range(1, 4):
        c1 = remote(hs.at[lax.rem(x + d, 4)], rs1.at[d - 1], q_send.at[d], q_recv.at[d], peer("x", d))
        c1.start()
        cx.append(c1)
    move3(1, (0, 1, 2))
    move4(3, (0, 1, 2))
    move4(2, (0, 1, 2))
    v = hs[x]
    for d in range(3):
        cx[d].wait()
        v = v + rs1[d]
    ts[...] = v
    at_last, at_zero = dp == 15, jnp.logical_and(dp == 0, core == 0)
    is_last, is_zero = me == 127, me == 0
    to_last = remote(ts, far_last.at[dp], qr_send.at[0], root_sem.at[0], (15, nw))
    to_zero = remote(ts, far_zero.at[dp], qr_send.at[1], root_sem.at[1], (0, nw))
    sends_zero = jnp.logical_and(core == 0, dp != 0)

    @pl.when(dp != 15)
    def _():
        to_last.start()

    @pl.when(sends_zero)
    def _():
        to_zero.start()

    move4(1, (0, 1, 2))
    in_last = remote(hn.at[0], near_last.at[nw], qr_send.at[2], root_sem.at[2], (15, 7))
    in_zero = remote(hn.at[1], near_zero.at[x], qr_send.at[3], root_sem.at[3], (0, 0))

    @pl.when(at_last)
    def _():
        pltpu.make_async_copy(far_last.at[0:15], far_last.at[0:15], root_sem.at[0]).wait()
        v = ts[...]
        for i in range(15):
            v = v + far_last[i]
        hn[0] = v

        @pl.when(nw != 7)
        def _():
            in_last.start()

        @pl.when(nw == 7)
        def _():
            near_last[7] = v

    @pl.when(at_zero)
    def _():
        pltpu.make_async_copy(far_zero.at[1:16], far_zero.at[1:16], root_sem.at[1]).wait()
        v = ts[...]
        for i in range(1, 16):
            v = v + far_zero[i]
        hn[1] = v

        @pl.when(x != 0)
        def _():
            in_zero.start()

        @pl.when(x == 0)
        def _():
            near_zero[0] = v

    low = first_tile(me)
    high = jnp.minimum(lax.div(SHARD * me + SHARD - 1 + 3072, 8192) - 1, 511)

    for s in range(6):
        @pl.when(jnp.logical_and(low + s >= 0, low + s <= high))
        def _(s=s):
            pltpu.make_async_copy(own.at[s], own.at[s], own_sem.at[s]).wait()
            for c in range(4):
                fl[pl.ds(64 * s + c, 16, stride=4), :] = own[s, c].astype(F32)

    @pl.when(is_last)
    def _():
        pltpu.make_async_copy(near_last.at[0:7], near_last.at[0:7], root_sem.at[2]).wait()
        for c in range(4):
            for h in range(2):
                sm4[c, 16 * h : 16 * h + 16, :] = near_last[2 * c + h]
            fl[pl.ds(192 + c, 21, stride=4), :] = sm4[c, 10:31, :]

    @pl.when(is_zero)
    def _():
        pltpu.make_async_copy(near_zero.at[1:4], near_zero.at[1:4], root_sem.at[3]).wait()
        for c in range(4):
            sm4[c, 0:16, :] = near_zero[c]
            fl[pl.ds(24 + c, 10, stride=4), :] = sm4[c, 0:10, :]

    offset = SHARD * me - C * (10 + 16 * low)
    row = lax.div(offset, 128)
    turn = lax.rem(offset, 128)
    back = lax.rem(128 - turn, 128)
    upper = pltpu.roll(fl[pl.ds(row, 264), :], back, 1)
    lower = pltpu.roll(fl[pl.ds(row + 1, 264), :], back, 1)
    lane = lax.broadcasted_iota(jnp.int32, (264, 128), 1)
    out[...] = jnp.where(lane < 128 - turn, upper, lower)

    for l in range(1, 7):
        for k, u, o in units(l):
            if l <= 2:
                copy0(l, k, u).wait_send()
            elif k >= taps[l - 2]:
                copy0(l, k, u).wait_send()
            whole(r1.at[u], s1_sem.at[u], r1_sem.at[u], o[0]).wait_send()
            whole(r2.at[u], s2_sem.at[u], r2_sem.at[u], o[1]).wait_send()
            whole(r3.at[u], s3_sem.at[u], r3_sem.at[u], o[2]).wait_send()
            tile, targets = owners(u)
            for i, (d, wanted) in enumerate(targets):
                @pl.when(jnp.logical_and(wanted, d != me))
                def _(u=u, i=i, tile=tile, d=d):
                    final(u, i, tile, d).wait_send()

    @pl.when(dp != 15)
    def _():
        to_last.wait_send()

    @pl.when(sends_zero)
    def _():
        to_zero.wait_send()

    @pl.when(jnp.logical_and(at_last, nw != 7))
    def _():
        in_last.wait_send()

    @pl.when(jnp.logical_and(at_zero, x != 0))
    def _():
        in_zero.wait_send()


def comm_scratch():
    dma = pltpu.SemaphoreType.DMA
    return [
        pltpu.VMEM((32, C), F32),
        pltpu.VMEM((2, 144, 128), BF),
        pltpu.VMEM((8, 144, 128), BF),
        pltpu.VMEM((7, 144, 128), BF),
        pltpu.VMEM((440, 128), F32),
        pltpu.VMEM((6, 4, 4, 4, 16, 128), BF),
        pltpu.VMEM((16, 4, 4, 4, 16, 128), BF),
        pltpu.VMEM((16, 4, 4, 4, 16, 128), BF),
        pltpu.VMEM((16, 3, 4, 4, 16, 128), BF),
        pltpu.VMEM((16, 4, 4, 16, 128), BF),
        pltpu.VMEM((16, 3, 4, 16, 128), BF),
        pltpu.VMEM((16, 4, 16, 128), BF),
        pltpu.VMEM((16, 3, 16, 128), BF),
        pltpu.VMEM((16, 16, 128), BF),
        pltpu.VMEM((6, 4, 16, 128), BF),
        pltpu.VMEM((392, 128), F32),
        pltpu.VMEM((16, C), F32),
        pltpu.VMEM((4, 16, 128), F32),
        pltpu.VMEM((3, 16, 128), F32),
        pltpu.VMEM((16, 128), F32),
        pltpu.VMEM((16, 16, 128), F32),
        pltpu.VMEM((16, 16, 128), F32),
        pltpu.VMEM((2, 16, 128), F32),
        pltpu.VMEM((8, 16, 128), F32),
        pltpu.VMEM((4, 16, 128), F32),
        pltpu.VMEM((4, 32, 128), F32),
        dma((7,)), dma((7,)),
        dma((16,)), dma((16,)), dma((16,)), dma((16,)), dma((16,)), dma((16,)), dma((16,)), dma((16,)),
        dma((16, 2)), dma((6,)),
        dma((4,)), dma((4,)), dma((4,)), dma((4,)),
    ]


def encoder_call(packed, cnt, bal, cot, w1, w3, w2, bias, gain, shift):
    vm = pl.BlockSpec(memory_space=pltpu.VMEM)
    sm = pl.BlockSpec(memory_space=pltpu.SMEM)
    hb = pl.BlockSpec(memory_space=pl.ANY)
    return pl.pallas_call(
        encoder_kernel,
        out_shape=jax.ShapeDtypeStruct((264, 128), F32),
        in_specs=[vm, sm, sm, vm, vm, hb, hb, vm, vm, vm],
        out_specs=vm,
        scratch_shapes=body_scratch() + comm_scratch(),
        compiler_params=pltpu.CompilerParams(
            vmem_limit_bytes=64 * 1024 * 1024 - 1024 * 64, collective_id=0, has_side_effects=True
        ),
    )(packed, cnt, bal, cot, w1, w3, w2, bias, gain, shift)


def pack_waves(waves):
    r = jnp.pad(waves.reshape(2, 400, 40), ((0, 0), (0, 32), (0, 0)))
    r = r.reshape(2, 3, 144, 40).transpose(0, 2, 1, 3).reshape(2, 144, 120)
    return jnp.pad(r, ((0, 0), (0, 0), (0, 8)))


def on_device(waveforms, valid_counts, balance_list, cotangent, w_first, w_three, w_two, conv_bias, norm_gain, norm_shift):
    shard = encoder_call(
        pack_waves(waveforms), valid_counts, balance_list, cotangent, w_first,
        w_three.reshape(4, 3 * C, C), w_two.reshape(2, 2 * C, C), conv_bias, norm_gain, norm_shift,
    )
    return shard.reshape(-1)[:SHARD]


def solution(mesh):
    both = ("dp", "narrow")
    in_specs = (
        P(both, None), P(both), P(both), P(both, None, None),
        P(), P(), P(), P(), P(), P(),
    )
    return jax.shard_map(on_device, mesh=mesh, in_specs=in_specs, out_specs=P(both), check_vma=False)
```
